32 devices in a mesh: aa: 8 (over z, x), ba: 4 (over y, core).
Axes of the slice: x: 2, y: 2, z: 4, core: 2. Of those that a mesh axis runs over, the one named last changes fastest.
Arguments:
- acts_a: bfloat16 [256, 28672], P('ba', 'aa'), may hold values from -13 to 13, as said below
- acts_b: bfloat16 [256, 28672], P('aa', 'ba'), may hold values from -13 to 13, as said below
Outputs:
- potential_a: float32 [28672], P('aa')
- potential_b: float32 [28672], P('ba')
The draws below stay inside these ranges and needn't reach their ends.
Inputs may be any that keep to these rules, and one draw needn't show every extreme that they name: `acts_a`: activations of order one with unit scales that differ from unit to unit. `acts_b`: activations of order one with unit scales that differ from unit to unit.
All inputs are finite; a program needn't handle non-finite values.
Results may differ from the reference program's by a relative error of at most 0.0003.
Values may be sent and summed in bfloat16 or wider, within the bound.
No kernel may reach another device: no remote copies, remote signals or barrier semaphores. Data moves between devices by JAX's collectives and lax.ppermute only.
A program may use at most 128 MiB of HBM per device.

```python
import math
import jax
import jax.numpy as jnp
from jax import lax

NA = 28672
NB = 28672
TOKENS = 256
ITERS = 2


def shared_base(key):
    return jnp.clip(jax.random.normal(key, (TOKENS, NA), jnp.float32), -6.0, 6.0)


def draw_acts_a(key, part):
    base = shared_base(key)
    key = jax.random.fold_in(key, 11)
    scales = jnp.exp(jax.random.uniform(key, (NA,), jnp.float32, jnp.log(0.5), jnp.log(2.0)))
    return (base * scales[None, :]).astype(jnp.bfloat16)


def draw_acts_b(key, part):
    base = shared_base(key)
    key = jax.random.fold_in(key, 23)
    first, second, third = jax.random.split(key, 3)
    scales = jnp.exp(jax.random.uniform(first, (NB,), jnp.float32, jnp.log(0.5), jnp.log(2.0)))
    order = jax.random.permutation(third, NB)
    matched = jnp.take(base, order, axis=1)
    noise = jnp.clip(jax.random.normal(second, (TOKENS, NB), jnp.float32), -6.0, 6.0)
    mixed = 0.6 * matched + 0.8 * noise
    return (mixed * scales[None, :]).astype(jnp.bfloat16)


def setup_inputs(seed: int = 0) -> dict:
    keys = jax.random.split(jax.random.key(seed), 3)
    acts_a = draw_acts_a(jax.random.fold_in(keys[2], 71), 0)
    acts_b = draw_acts_b(jax.random.fold_in(keys[2], 71), 0)
    return dict(acts_a=acts_a, acts_b=acts_b)


epsilon = 0.01


def combine(first, second):
    upper = jnp.maximum(first[0], second[0])
    return (upper, first[1] * jnp.exp(first[0] - upper) + second[1] * jnp.exp(second[0] - upper))


def cost_rows(acts_a, acts_b, norm_a, norm_b, start, block):
    rows = lax.dynamic_slice_in_dim(acts_a, start, block, 1)
    cross = lax.dot_general(rows, acts_b, (((0,), (0,)), ((), ())), preferred_element_type=jnp.float32)
    norms = lax.dynamic_slice_in_dim(norm_a, start, block, 0)
    return (norms[:, None] + norm_b[None, :] - 2.0 * cross) / TOKENS


def reference(acts_a, acts_b):
    block = min(512, NA)
    count = NA // block
    norm_a = jnp.sum(jnp.square(acts_a.astype(jnp.float32)), 0)
    norm_b = jnp.sum(jnp.square(acts_b.astype(jnp.float32)), 0)
    potential_b = jnp.zeros((NB,), jnp.float32)
    potential_a = jnp.zeros((NA,), jnp.float32)
    for step in range(ITERS):
        def row_part(index):
            cost = cost_rows(acts_a, acts_b, norm_a, norm_b, index * block, block)
            scores = (potential_b[None, :] - cost) / epsilon
            upper = jnp.max(scores, 1)
            return upper + jnp.log(jnp.sum(jnp.exp(scores - upper[:, None]), 1))
        lse_rows = lax.map(row_part, jnp.arange(count, dtype=jnp.int32)).reshape(NA)
        potential_a = -epsilon * math.log(NA) - epsilon * lse_rows

        def col_part(carry, index):
            cost = cost_rows(acts_a, acts_b, norm_a, norm_b, index * block, block)
            part_a = lax.dynamic_slice_in_dim(potential_a, index * block, block, 0)
            scores = (part_a[:, None] - cost) / epsilon
            upper = jnp.max(scores, 0)
            total = jnp.sum(jnp.exp(scores - upper[None, :]), 0)
            return combine(carry, (upper, total)), None
        start = (jnp.full((NB,), -jnp.inf, jnp.float32), jnp.zeros((NB,), jnp.float32))
        (upper, total), unused = lax.scan(col_part, start, jnp.arange(count, dtype=jnp.int32))
        potential_b = -epsilon * math.log(NB) - epsilon * (upper + jnp.log(total))
    return potential_a, potential_b
```

```python
import functools
import math

import jax
import jax.numpy as jnp
from jax import lax
from jax.experimental import pallas as pl
from jax.experimental.pallas import tpu as pltpu
from jax.sharding import PartitionSpec as P

NA = 28672
NB = 28672
TOKENS = 256
epsilon = 0.01

f32 = jnp.float32
bf16 = jnp.bfloat16
VMEM = pl.BlockSpec(memory_space=pltpu.VMEM)

KAPPA = math.log2(math.e) * 2.0 / (TOKENS * epsilon)
LN2 = math.log(2.0)
SMALLEST = 2.0**-60


def params(mib):
    return pltpu.CompilerParams(vmem_limit_bytes=mib << 20)


def largest_tile(size, *options):
    for tile in options:
        if size % tile == 0:
            return tile
    return size


def lse_kernel(tm, tn, keep, lhs_ref, rhs_ref, bias_ref, max_in, sum_in, max_ref, sum_ref, *rest):
    if keep:
        tile_max_ref, kept_ref, first_block, second_block = rest
    else:
        first_block, second_block = rest
    blocks = (first_block, second_block)
    row_tiles = lhs_ref.shape[0] // tm
    total = row_tiles * (rhs_ref.shape[1] // tn)
    sub = 64
    lanes = tn // 128

    def cols(n):
        return pl.ds(pl.multiple_of(n * tn, tn), tn)

    def product(n, t, block):
        rows = pl.ds(pl.multiple_of(t * tm, tm), tm)
        block[...] = jnp.dot(lhs_ref[rows, :], rhs_ref[:, cols(n)], preferred_element_type=f32)

    def reduce(n, t, block, upper, total_sum):
        new = upper
        for k in range(tm // sub):
            rows = pl.ds(pl.multiple_of(t * tm + k * sub, sub), sub)
            bias = jnp.concatenate([bias_ref[rows, :]] * lanes, 1)
            x = block[k * sub : (k + 1) * sub, :] + bias
            block[k * sub : (k + 1) * sub, :] = x
            new = jnp.maximum(new, x.reshape(sub // 8, 8, tn).max(0))
        row = new.max(0, keepdims=True)
        new = jnp.broadcast_to(row, (8, tn))
        total_sum = total_sum * jnp.exp2((upper - new) * KAPPA)
        for k in range(tm // sub):
            rows = pl.ds(pl.multiple_of(t * tm + k * sub, sub), sub)
            p = jnp.exp2((block[k * sub : (k + 1) * sub, :] - row) * KAPPA)
            total_sum = total_sum + p.reshape(sub // 8, 8, tn).sum(0)
            if keep:
                kept_ref[rows, cols(n)] = p.astype(bf16)
        if keep:
            tile_max_ref[pl.ds(t, 1), cols(n)] = row
        return new, total_sum

    product(0, 0, first_block)

    def pair(k, carry):
        upper, total_sum = carry
        for half in range(2):
            step = 2 * k + half
            n = step // row_tiles
            t = step - n * row_tiles
            after = jnp.minimum(step + 1, total - 1)
            n_after = after // row_tiles
            upper = jnp.where(t == 0, jnp.broadcast_to(max_in[:, cols(n)], (8, tn)), upper)
            total_sum = jnp.where(t == 0, sum_in[:, cols(n)], total_sum)
            product(n_after, after - n_after * row_tiles, blocks[1 - half])
            upper, total_sum = reduce(n, t, blocks[half], upper, total_sum)
            max_ref[:, cols(n)] = upper[:1]
            sum_ref[:, cols(n)] = total_sum
        return upper, total_sum

    zeros = jnp.zeros((8, tn), f32)
    lax.fori_loop(0, total // 2, pair, (zeros, zeros))


def lse_start(n):
    return (jnp.full((1, n), -1e30, f32), jnp.zeros((8, n), f32))


def lse_call(lhs, rhs, bias, state, keep):
    m, n = lhs.shape[0], rhs.shape[1]
    tm = largest_tile(m, 896)
    tn = largest_tile(n, 512, 256)
    outs = [jax.ShapeDtypeStruct((1, n), f32), jax.ShapeDtypeStruct((8, n), f32)]
    if keep:
        outs += [jax.ShapeDtypeStruct((m // tm, n), f32), pltpu.VMEM((m, n), bf16)]
    bias = jnp.broadcast_to(bias[:, None], (m, 128))
    return pl.pallas_call(
        functools.partial(lse_kernel, tm, tn, keep),
        out_shape=outs,
        in_specs=[VMEM] * 5,
        out_specs=[VMEM] * len(outs),
        scratch_shapes=[pltpu.VMEM((tm, tn), f32)] * 2,
        compiler_params=params(13 if keep else 20),
    )(lhs, rhs, bias, *state)


def row_sum_kernel(kept_ref, weight_ref, out_ref, wide, partial):
    rows_here, cols_here = kept_ref.shape
    tiles = weight_ref.shape[0]
    tm = rows_here // tiles
    lanes = cols_here // 128

    @pl.loop(0, tiles)
    def _(t):
        wide[...] = jnp.broadcast_to(weight_ref[pl.ds(t, 1), :], (16, cols_here)).astype(bf16)

        @pl.loop(0, tm // 32)
        def _(g):
            start = pl.multiple_of(t * tm + g * 32, 32)
            acc = [jnp.zeros((16, 128), f32)] * 2
            for c in range(0, lanes, 4):
                part = [None, None]
                for k in range(c, min(c + 4, lanes)):
                    w = wide[:, k * 128 : (k + 1) * 128]
                    for h in range(2):
                        term = kept_ref[pl.ds(start + h * 16, 16), k * 128 : (k + 1) * 128] * w
                        part[h] = term if part[h] is None else part[h] + term
                for h in range(2):
                    acc[h] = acc[h] + part[h].astype(f32)
            for h in range(2):
                partial[pl.ds(start + h * 16, 16), :] = acc[h]

    @pl.loop(0, rows_here // 128)
    def _(g):
        rows = pl.ds(pl.multiple_of(g * 128, 128), 128)
        out_ref[:, rows] = jnp.sum(partial[rows, :].T, axis=0, keepdims=True)


def row_sum_call(kept, weight):
    return pl.pallas_call(
        row_sum_kernel,
        out_shape=jax.ShapeDtypeStruct((1, kept.shape[0]), f32),
        in_specs=[VMEM] * 2,
        out_specs=VMEM,
        scratch_shapes=[pltpu.VMEM((16, kept.shape[1]), bf16), pltpu.VMEM((kept.shape[0], 128), f32)],
        compiler_params=params(10),
    )(kept, weight)


def col_sum_kernel(kept_ref, weight_ref, scale_ref, out_ref):
    rows_here, cols_here = kept_ref.shape
    tiles = weight_ref.shape[0]
    tm = rows_here // tiles
    width = 512 if cols_here % 512 == 0 else 256

    @pl.loop(0, cols_here // width)
    def _(n):
        start = pl.multiple_of(n * width, width)

        def tile(t, total):
            def group(g, acc):
                acc = list(acc)
                first = pl.multiple_of(t * tm + g * 64, 64)
                scale = [scale_ref[pl.ds(first + h * 16, 16), :] for h in range(4)]
                for k in range(width // 128):
                    part = None
                    for h in range(4):
                        cols = pl.ds(pl.multiple_of(start + k * 128, 128), 128)
                        term = kept_ref[pl.ds(first + h * 16, 16), cols] * scale[h]
                        part = term if part is None else part + term
                    acc[k] = acc[k] + part.astype(f32)
                return tuple(acc)

            acc = lax.fori_loop(0, tm // 64, group, (jnp.zeros((16, 128), f32),) * (width // 128), unroll=2)
            acc = jnp.concatenate(acc, 1)
            return total + jnp.sum(acc, 0, keepdims=True) * weight_ref[pl.ds(t, 1), pl.ds(start, width)]

        out_ref[:, pl.ds(start, width)] = lax.fori_loop(0, tiles, tile, jnp.zeros((1, width), f32))


def col_sum_call(kept, weight, scale):
    wide = jnp.broadcast_to(scale.astype(bf16)[:, None], (scale.shape[0], 128))
    return pl.pallas_call(
        col_sum_kernel,
        out_shape=jax.ShapeDtypeStruct((1, kept.shape[1]), f32),
        in_specs=[VMEM] * 3,
        out_specs=VMEM,
        compiler_params=params(10),
    )(kept, weight, wide)


def group_steps(axis, size):
    step = 1
    while step < size:
        yield lambda x, s=step: lax.ppermute(x, axis, [(i, i ^ s) for i in range(size)])
        step *= 2


def group_lse(upper, total, exchange_steps):
    pair = jnp.stack([upper, total])
    for exchange in exchange_steps:
        other = exchange(pair)
        top = jnp.maximum(pair[0], other[0])
        total = pair[1] * jnp.exp2((pair[0] - top) * KAPPA) + other[1] * jnp.exp2((other[0] - top) * KAPPA)
        pair = jnp.stack([top, total])
    return KAPPA * pair[0] + jnp.log2(pair[1])


def group_sum(x, exchange_steps):
    for exchange in exchange_steps:
        x = x + exchange(x)
    return x


def per_device(aa_size, ba_size, acts_a, acts_b):
    def over_a():
        return group_steps("aa", aa_size)

    def over_b():
        return group_steps("ba", ba_size)

    whole_a = lax.all_gather(acts_a, "ba", axis=0, tiled=True)
    whole_b = lax.all_gather(acts_b, "aa", axis=0, tiled=True)
    turned_a = whole_a.T
    turned_b = whole_b.T
    norm_a = jnp.sum(jnp.square(whole_a.astype(f32)), 0)
    norm_b = jnp.sum(jnp.square(whole_b.astype(f32)), 0)
    rows_here, cols_here = norm_a.shape[0], norm_b.shape[0]
    log_n = math.log(NA)

    def row_pass(bias):
        upper, total = lse_call(turned_b, whole_a, bias, lse_start(rows_here), False)
        return group_lse(upper[0], total.sum(0), over_b())

    def potential_a_of(row_lse):
        return -epsilon * (log_n + LN2 * (row_lse - (0.5 * KAPPA) * norm_a))

    def potential_b_of(col_lse):
        return -epsilon * LN2 * (col_lse - (0.5 * KAPPA) * norm_b)

    row_lse = row_pass(-0.5 * norm_b)
    upper, total, tile_max, kept = lse_call(
        turned_a, whole_b, row_lse * (-1.0 / KAPPA), lse_start(cols_here), True
    )
    col_lse = group_lse(upper[0], total.sum(0), over_a())
    weight = jnp.exp2(KAPPA * tile_max - col_lse[None, :])
    kept = pltpu.with_memory_space_constraint(kept, pltpu.VMEM)
    row_sums = group_sum(row_sum_call(kept, weight)[0], over_b())
    low = jnp.min(row_sums) < SMALLEST
    safe = jnp.maximum(row_sums, SMALLEST)
    col_sums = col_sum_call(kept, weight, 1.0 / safe)[0]
    flagged = jnp.concatenate([col_sums, jnp.where(low, jnp.ones((128,), f32), 0.0)])
    flagged = group_sum(flagged, over_a())
    col_sums = flagged[:cols_here]

    def quick(_):
        return (
            potential_a_of(row_lse) - epsilon * jnp.log(safe),
            potential_b_of(col_lse) - epsilon * jnp.log(col_sums),
        )

    def exact(_):
        again = row_pass(col_lse * (-1.0 / KAPPA))
        upper, total = lse_call(
            turned_a, whole_b, again * (-1.0 / KAPPA), lse_start(cols_here), False
        )
        return potential_a_of(again), potential_b_of(group_lse(upper[0], total.sum(0), over_a()))

    return lax.cond(flagged[cols_here] > 0.0, exact, quick, 0)


def solution(mesh):
    in_specs = (P("ba", "aa"), P("aa", "ba"))
    out_specs = (P("aa"), P("ba"))
    return jax.shard_map(
        functools.partial(per_device, mesh.shape["aa"], mesh.shape["ba"]),
        mesh=mesh, in_specs=in_specs, out_specs=out_specs, check_vma=False,
    )
```

```python
import functools
import math

import jax
import jax.numpy as jnp
from jax import lax
from jax.experimental import pallas as pl
from jax.experimental.pallas import tpu as pltpu
from jax.sharding import PartitionSpec as P

NA = 28672
NB = 28672
TOKENS = 256
epsilon = 0.01

f32 = jnp.float32
bf16 = jnp.bfloat16
VMEM = pl.BlockSpec(memory_space=pltpu.VMEM)

KAPPA = math.log2(math.e) * 2.0 / (TOKENS * epsilon)
LN2 = math.log(2.0)
SMALLEST = 2.0**-60


def params(mib):
    return pltpu.CompilerParams(vmem_limit_bytes=mib << 20)


def lse_kernel(tm, tn, biased, chained, keep, lhs_ref, rhs_ref, *rest):
    rest = list(rest)
    bias_ref = rest.pop(0) if biased else None
    state_in = rest.pop(0) if chained else None
    state_ref = rest.pop(0)
    norm_ref = None if biased else rest.pop(0)
    if keep:
        tile_max_ref, kept_ref = rest.pop(0), rest.pop(0)
    turned, wide, *blocks = rest
    row_tiles = lhs_ref.shape[1] // tm
    total = row_tiles * (rhs_ref.shape[1] // tn)
    sub = 64
    lanes = tn // 128

    @pl.loop(0, lhs_ref.shape[1] // 128)
    def _(g):
        rows = pl.ds(pl.multiple_of(g * 128, 128), 128)
        turned[rows, :] = lhs_ref[:, rows].T
        if biased:
            bias = bias_ref[:, rows]
        else:
            norm = jnp.sum(jnp.square(lhs_ref[:, rows].astype(f32)), 0, keepdims=True)
            norm_ref[:, rows] = norm
            bias = -0.5 * norm
        wide[rows, :] = jnp.broadcast_to(bias, (128, 128)).T

    def cols(n):
        return pl.ds(pl.multiple_of(n * tn, tn), tn)

    def product(n, t, block):
        rows = pl.ds(pl.multiple_of(t * tm, tm), tm)
        block[...] = jnp.dot(turned[rows, :], rhs_ref[:, cols(n)], preferred_element_type=f32)

    def reduce(n, t, block, upper, total_sum):
        new = upper
        for k in range(tm // sub):
            rows = pl.ds(pl.multiple_of(t * tm + k * sub, sub), sub)
            bias = jnp.concatenate([wide[rows, :]] * lanes, 1)
            x = block[k * sub : (k + 1) * sub, :] + bias
            block[k * sub : (k + 1) * sub, :] = x
            new = jnp.maximum(new, x.reshape(sub // 8, 8, tn).max(0))
        row = new.max(0, keepdims=True)
        new = jnp.broadcast_to(row, (8, tn))
        total_sum = total_sum * jnp.exp2((upper - new) * KAPPA)
        for k in range(tm // sub):
            rows = pl.ds(pl.multiple_of(t * tm + k * sub, sub), sub)
            p = jnp.exp2((block[k * sub : (k + 1) * sub, :] - row) * KAPPA)
            total_sum = total_sum + p.reshape(sub // 8, 8, tn).sum(0)
            if keep:
                kept_ref[rows, cols(n)] = p.astype(bf16)
        if keep:
            tile_max_ref[pl.ds(t, 1), cols(n)] = row
        return new, total_sum

    product(0, 0, blocks[0])
    first_sublane = lax.broadcasted_iota(jnp.int32, (8, tn), 0) == 0

    def pair(k, carry):
        upper, total_sum = carry
        for half in range(2):
            step = 2 * k + half
            n = step // row_tiles
            t = step - n * row_tiles
            after = jnp.minimum(step + 1, total - 1)
            n_after = after // row_tiles
            if chained:
                start = state_in[:, cols(n)]
                start_max = jnp.broadcast_to(start[:1], (8, tn))
                start_sum = jnp.where(first_sublane, jnp.broadcast_to(start[1:], (8, tn)), 0.0)
            else:
                start_max, start_sum = jnp.full((8, tn), -1e30, f32), jnp.zeros((8, tn), f32)
            upper = jnp.where(t == 0, start_max, upper)
            total_sum = jnp.where(t == 0, start_sum, total_sum)
            product(n_after, after - n_after * row_tiles, blocks[1 - half])
            upper, total_sum = reduce(n, t, blocks[half], upper, total_sum)
            state_ref[0:1, cols(n)] = upper[:1]
            state_ref[1:2, cols(n)] = jnp.sum(total_sum, 0, keepdims=True)
        return upper, total_sum

    zeros = jnp.zeros((8, tn), f32)
    lax.fori_loop(0, total // 2, pair, (zeros, zeros))


def lse_call(lhs, rhs, bias=None, state=None, keep=False):
    depth, m = lhs.shape
    n = rhs.shape[1]
    tm, tn = (896, 512) if n % 512 == 0 else (448, 896)
    outs = [jax.ShapeDtypeStruct((2, n), f32)]
    operands = [lhs, rhs]
    if bias is None:
        outs += [jax.ShapeDtypeStruct((1, m), f32)]
    else:
        operands += [bias]
    if state is not None:
        operands += [state]
    if keep:
        outs += [jax.ShapeDtypeStruct((m // tm, n), f32), pltpu.VMEM((m, n), bf16)]
    return pl.pallas_call(
        functools.partial(lse_kernel, tm, tn, bias is not None, state is not None, keep),
        out_shape=outs,
        in_specs=[VMEM] * len(operands),
        out_specs=[VMEM] * len(outs),
        scratch_shapes=[pltpu.VMEM((m, depth), bf16), pltpu.VMEM((m, 128), f32)]
        + [pltpu.VMEM((tm, tn), f32)] * 2,
        compiler_params=params(12),
        cost_estimate=pl.CostEstimate(flops=512 * m * n, bytes_accessed=512 * (m + n), transcendentals=m * n),
    )(*operands)


def reorder_kernel(tokens, table_ref, arrived_ref, out_ref, norm_ref):
    for p in range(table_ref.shape[0]):
        start = pl.multiple_of(table_ref[p] * tokens, tokens)
        out_ref[p * tokens : (p + 1) * tokens, :] = arrived_ref[pl.ds(start, tokens), :]

    @pl.loop(0, arrived_ref.shape[1] // 128)
    def _(g):
        cols = pl.ds(pl.multiple_of(g * 128, 128), 128)
        norm_ref[:, cols] = jnp.sum(jnp.square(arrived_ref[:, cols].astype(f32)), 0, keepdims=True)


def reorder_call(arrived, table, tokens):
    return pl.pallas_call(
        functools.partial(reorder_kernel, tokens),
        out_shape=[
            jax.ShapeDtypeStruct(arrived.shape, bf16),
            jax.ShapeDtypeStruct((1, arrived.shape[1]), f32),
        ],
        in_specs=[pl.BlockSpec(memory_space=pltpu.SMEM), VMEM],
        out_specs=[VMEM] * 2,
        compiler_params=params(8),
    )(table, arrived)


def weights(tile_max_ref, lse_ref, t):
    return jnp.exp2(KAPPA * tile_max_ref[pl.ds(t, 1), :] - lse_ref[...])


def row_sum_kernel(chained, kept_ref, tile_max_ref, lse_ref, *rest):
    rest = list(rest)
    first = rest.pop(0) if chained else None
    out_ref, wide, partial = rest
    rows_here, cols_here = kept_ref.shape
    tiles = tile_max_ref.shape[0]
    tm = rows_here // tiles
    span, lane_block, height = 1024, 256, 64

    @pl.loop(0, tiles)
    def _(t):
        wide[...] = jnp.broadcast_to(weights(tile_max_ref, lse_ref, t), (16, cols_here)).astype(bf16)

        @pl.loop(0, tm // height)
        def _(g):
            rows = pl.ds(pl.multiple_of(t * tm + g * height, height), height)
            acc = jnp.zeros((height, 128), f32)
            for c in range(0, cols_here, span):
                part = None
                for k in range(c, min(c + span, cols_here), lane_block):
                    w = jnp.concatenate([wide[:, k : k + lane_block]] * (height // 16), 0)
                    term = kept_ref[rows, k : k + lane_block] * w
                    part = term if part is None else part + term
                part = part.astype(f32)
                for k in range(0, lane_block, 128):
                    acc = acc + part[:, k : k + 128]
            partial[rows, :] = acc

    @pl.loop(0, rows_here // 128)
    def _(g):
        rows = pl.ds(pl.multiple_of(g * 128, 128), 128)
        total = jnp.sum(partial[rows, :].T, axis=0, keepdims=True)
        out_ref[:, rows] = first[:, rows] + total if chained else total


def row_sum_call(kept, tile_max, lse, first=None):
    operands = (kept, tile_max, lse) if first is None else (kept, tile_max, lse, first)
    m, n = kept.shape
    return pl.pallas_call(
        functools.partial(row_sum_kernel, first is not None),
        out_shape=jax.ShapeDtypeStruct((1, m), f32),
        in_specs=[VMEM] * len(operands),
        out_specs=VMEM,
        scratch_shapes=[pltpu.VMEM((16, n), bf16), pltpu.VMEM((m, 128), f32)],
        compiler_params=params(6),
        cost_estimate=pl.CostEstimate(flops=2 * m * n, bytes_accessed=2 * m * n, transcendentals=0),
    )(*operands)


def col_sum_kernel(kept_ref, tile_max_ref, lse_ref, row_sum_ref, out_ref, wide):
    rows_here, cols_here = kept_ref.shape
    tiles = tile_max_ref.shape[0]
    tm = rows_here // tiles
    width = 896

    @pl.loop(0, rows_here // 128)
    def _(g):
        rows = pl.ds(pl.multiple_of(g * 128, 128), 128)
        scale = 1.0 / jnp.maximum(row_sum_ref[:, rows], SMALLEST)
        wide[rows, :] = jnp.broadcast_to(scale, (128, 128)).T.astype(bf16)

    least = jnp.min(row_sum_ref[...], axis=1, keepdims=True)
    out_ref[:, cols_here:] = jnp.broadcast_to(jnp.where(least < SMALLEST, 1.0, 0.0), (1, 128))

    @pl.loop(0, cols_here // width)
    def _(n):
        start = pl.multiple_of(n * width, 128)

        def tile(t, total):
            acc = jnp.zeros((16, width), f32)
            for g in range(tm // 64):
                part = None
                for h in range(4):
                    rows = pl.ds(pl.multiple_of(t * tm + g * 64 + h * 16, 16), 16)
                    scale = jnp.concatenate([wide[rows, :]] * (width // 128), 1)
                    term = kept_ref[rows, pl.ds(start, width)] * scale
                    part = term if part is None else part + term
                acc = acc + part.astype(f32)
            acc = jnp.sum(acc, 0, keepdims=True)
            cols = pl.ds(start, width)
            return total + acc * jnp.exp2(KAPPA * tile_max_ref[pl.ds(t, 1), cols] - lse_ref[:, cols])

        out_ref[:, pl.ds(start, width)] = lax.fori_loop(0, tiles, tile, jnp.zeros((1, width), f32))


def col_sum_call(kept, tile_max, lse, row_sums):
    m, n = kept.shape
    return pl.pallas_call(
        col_sum_kernel,
        out_shape=jax.ShapeDtypeStruct((1, n + 128), f32),
        in_specs=[VMEM] * 4,
        out_specs=VMEM,
        scratch_shapes=[pltpu.VMEM((m, 128), bf16)],
        compiler_params=params(6),
        cost_estimate=pl.CostEstimate(flops=2 * m * n, bytes_accessed=2 * m * n, transcendentals=0),
    )(kept, tile_max, lse, row_sums)


def group_steps(axis, size):
    step = 1
    while step < size:
        yield lambda x, s=step: lax.ppermute(x, axis, [(i, i ^ s) for i in range(size)])
        step *= 2


def group_lse(pair, exchange_steps):
    for exchange in exchange_steps:
        other = exchange(pair)
        top = jnp.maximum(pair[:1], other[:1])
        total = pair[1:] * jnp.exp2((pair[:1] - top) * KAPPA) + other[1:] * jnp.exp2((other[:1] - top) * KAPPA)
        pair = jnp.concatenate([top, total], 0)
    return KAPPA * pair[:1] + jnp.log2(pair[1:])


def group_sum(x, exchange_steps):
    for exchange in exchange_steps:
        x = x + exchange(x)
    return x


def swap(x, axis, size, mask):
    return lax.ppermute(x, axis, [(i, i ^ mask) for i in range(size)])


def gather_order(size, near):
    far = size // near
    return [f * near + k for k in range(near) for f in range(far)]


def gather_near(x, axis, size, near):
    mine = jnp.concatenate([x] + [swap(x, axis, size, f * near) for f in range(1, size // near)], 0)
    return jnp.concatenate([mine] + [swap(mine, axis, size, k) for k in range(1, near)], 0)


CHUNKS = 4
HALVES = 2


def per_device(aa_size, ba_size, acts_a, acts_b):
    def over_a():
        return group_steps("aa", aa_size)

    def over_b():
        return group_steps("ba", ba_size)

    cols_here = acts_b.shape[1]
    width = cols_here // CHUNKS
    half = cols_here // HALVES
    near = aa_size // 4
    far_masks = [f * near for f in range(1, 4)]

    tokens = acts_b.shape[0]
    per_block = aa_size // ba_size
    arrival = gather_order(ba_size, 2)
    place = jnp.array([arrival.index(v) for v in range(ba_size)], jnp.int32)
    token_block = lax.axis_index("aa") ^ jnp.array(gather_order(aa_size, near), jnp.int32)
    table = place[(token_block // per_block) ^ lax.axis_index("ba")] * per_block + token_block % per_block
    whole_a, norm_a = reorder_call(gather_near(acts_a, "ba", ba_size, 2), table, tokens)

    chunks, norms_b = [], []
    state = None
    states = []
    for c in range(CHUNKS):
        own = acts_b[:, c * width : (c + 1) * width]
        group = [own] + [swap(own, "aa", aa_size, mask) for mask in far_masks]
        if c >= 2:
            group, states[c - 2] = lax.optimization_barrier((group, states[c - 2]))
        mine = jnp.concatenate(group, 0)
        chunk = jnp.concatenate([mine] + [swap(mine, "aa", aa_size, k) for k in range(1, near)], 0)
        state, norm = lse_call(chunk, whole_a, None, states[c - 1] if c else None)
        states.append(state)
        chunks.append(chunk)
        norms_b.append(norm)
    row_lse = group_lse(states[-1], over_b())
    per_half = CHUNKS // HALVES
    norms_b = [jnp.concatenate(norms_b[h * per_half : (h + 1) * per_half], 1) for h in range(HALVES)]
    halves = [jnp.concatenate(chunks[h * per_half : (h + 1) * per_half], 1) for h in range(HALVES)]
    log_n = math.log(NA)

    def potential_a_of(row_lse):
        return -epsilon * (log_n + LN2 * (row_lse - (0.5 * KAPPA) * norm_a))

    def potential_b_of(col_lse, norm_b):
        return -epsilon * LN2 * (col_lse - (0.5 * KAPPA) * norm_b)

    col_lse, tile_max, kept = [], [], []
    for part in halves:
        state, top, p = lse_call(whole_a, part, row_lse * (-1.0 / KAPPA), keep=True)
        col_lse.append(group_lse(state, over_a()))
        tile_max.append(top)
        kept.append(pltpu.with_memory_space_constraint(p, pltpu.VMEM))
    row_sums = None
    for h in range(HALVES):
        row_sums = row_sum_call(kept[h], tile_max[h], col_lse[h], row_sums)
    row_sums = group_sum(row_sums, over_b())
    col_sums = []
    for h in range(HALVES):
        sums = col_sum_call(kept[h], tile_max[h], col_lse[h], row_sums)
        col_sums.append(group_sum(sums, over_a()))

    def quick(_):
        second_a = potential_a_of(row_lse) - epsilon * jnp.log(row_sums)
        second_b = [
            potential_b_of(col_lse[h], norms_b[h]) - epsilon * jnp.log(col_sums[h][:, :half])
            for h in range(HALVES)
        ]
        return second_a, jnp.concatenate(second_b, 1)

    def exact(_):
        state = None
        for part, lse in zip(halves, col_lse):
            (state,) = lse_call(part, whole_a, lse * (-1.0 / KAPPA), state)
        again = group_lse(state, over_b())
        second_b = []
        for part, norm_b in zip(halves, norms_b):
            (state,) = lse_call(whole_a, part, again * (-1.0 / KAPPA))
            second_b.append(potential_b_of(group_lse(state, over_a()), norm_b))
        return potential_a_of(again), jnp.concatenate(second_b, 1)

    second_a, second_b = lax.cond(col_sums[0][0, half] > 0.0, exact, quick, 0)
    return second_a.reshape(-1), second_b.reshape(-1)


def solution(mesh):
    in_specs = (P("ba", "aa"), P("aa", "ba"))
    out_specs = (P("aa"), P("ba"))
    return jax.shard_map(
        functools.partial(per_device, mesh.shape["aa"], mesh.shape["ba"]),
        mesh=mesh, in_specs=in_specs, out_specs=out_specs, check_vma=False,
    )
```

```python
import functools
import math

import jax
import jax.numpy as jnp
from jax import lax
from jax.experimental import pallas as pl
from jax.experimental.pallas import tpu as pltpu
from jax.sharding import PartitionSpec as P

NA = 28672
NB = 28672
TOKENS = 256
epsilon = 0.01

f32 = jnp.float32
bf16 = jnp.bfloat16
VMEM = pl.BlockSpec(memory_space=pltpu.VMEM)

KAPPA = math.log2(math.e) * 2.0 / (TOKENS * epsilon)
LN2 = math.log(2.0)
SMALLEST = 2.0**-60


def params(mib):
    return pltpu.CompilerParams(vmem_limit_bytes=mib << 20)


def lse_kernel(tm, tn, biased, chained, keep, lhs_ref, rhs_ref, *rest):
    rest = list(rest)
    bias_ref = rest.pop(0) if biased else None
    state_in = rest.pop(0) if chained else None
    state_ref = rest.pop(0)
    norm_ref = None if biased else rest.pop(0)
    if keep:
        tile_max_ref, kept_ref = rest.pop(0), rest.pop(0)
    turned, wide, *blocks = rest
    row_tiles = lhs_ref.shape[1] // tm
    total = row_tiles * (rhs_ref.shape[1] // tn)
    sub = 64
    lanes = tn // 128

    @pl.loop(0, lhs_ref.shape[1] // 128)
    def _(g):
        rows = pl.ds(pl.multiple_of(g * 128, 128), 128)
        turned[rows, :] = lhs_ref[:, rows].T
        if biased:
            bias = bias_ref[:, rows]
        else:
            norm = jnp.sum(jnp.square(lhs_ref[:, rows].astype(f32)), 0, keepdims=True)
            norm_ref[:, rows] = norm
            bias = -0.5 * norm
        wide[rows, :] = jnp.broadcast_to(bias, (128, 128)).T

    def cols(n):
        return pl.ds(pl.multiple_of(n * tn, tn), tn)

    def product(n, t, block):
        rows = pl.ds(pl.multiple_of(t * tm, tm), tm)
        block[...] = jnp.dot(turned[rows, :], rhs_ref[:, cols(n)], preferred_element_type=f32)

    def reduce(n, t, block, upper, total_sum):
        new = upper
        for k in range(tm // sub):
            rows = pl.ds(pl.multiple_of(t * tm + k * sub, sub), sub)
            bias = jnp.concatenate([wide[rows, :]] * lanes, 1)
            x = block[k * sub : (k + 1) * sub, :] + bias
            block[k * sub : (k + 1) * sub, :] = x
            new = jnp.maximum(new, x.reshape(sub // 8, 8, tn).max(0))
        row = new.max(0, keepdims=True)
        new = jnp.broadcast_to(row, (8, tn))
        total_sum = total_sum * jnp.exp2((upper - new) * KAPPA)
        for k in range(tm // sub):
            rows = pl.ds(pl.multiple_of(t * tm + k * sub, sub), sub)
            p = jnp.exp2((block[k * sub : (k + 1) * sub, :] - row) * KAPPA)
            total_sum = total_sum + p.reshape(sub // 8, 8, tn).sum(0)
            if keep:
                kept_ref[rows, cols(n)] = p.astype(bf16)
        if keep:
            tile_max_ref[pl.ds(t, 1), cols(n)] = row
        return new, total_sum

    product(0, 0, blocks[0])
    first_sublane = lax.broadcasted_iota(jnp.int32, (8, tn), 0) == 0

    def pair(k, carry):
        upper, total_sum = carry
        for half in range(2):
            step = 2 * k + half
            n = step // row_tiles
            t = step - n * row_tiles
            after = jnp.minimum(step + 1, total - 1)
            n_after = after // row_tiles
            if chained:
                start = state_in[:, cols(n)]
                start_max = jnp.broadcast_to(start[:1], (8, tn))
                start_sum = jnp.where(first_sublane, jnp.broadcast_to(start[1:], (8, tn)), 0.0)
            else:
                start_max, start_sum = jnp.full((8, tn), -1e30, f32), jnp.zeros((8, tn), f32)
            upper = jnp.where(t == 0, start_max, upper)
            total_sum = jnp.where(t == 0, start_sum, total_sum)
            product(n_after, after - n_after * row_tiles, blocks[1 - half])
            upper, total_sum = reduce(n, t, blocks[half], upper, total_sum)
            state_ref[0:1, cols(n)] = upper[:1]
            state_ref[1:2, cols(n)] = jnp.sum(total_sum, 0, keepdims=True)
        return upper, total_sum

    zeros = jnp.zeros((8, tn), f32)
    lax.fori_loop(0, total // 2, pair, (zeros, zeros))


def lse_call(lhs, rhs, bias=None, state=None, keep=False):
    depth, m = lhs.shape
    n = rhs.shape[1]
    tm, tn = (896, 512) if n % 512 == 0 else (448, 896)
    outs = [jax.ShapeDtypeStruct((2, n), f32)]
    operands = [lhs, rhs]
    if bias is None:
        outs += [jax.ShapeDtypeStruct((1, m), f32)]
    else:
        operands += [bias]
    if state is not None:
        operands += [state]
    if keep:
        outs += [jax.ShapeDtypeStruct((m // tm, n), f32), pltpu.VMEM((m, n), bf16)]
    return pl.pallas_call(
        functools.partial(lse_kernel, tm, tn, bias is not None, state is not None, keep),
        out_shape=outs,
        in_specs=[VMEM] * len(operands),
        out_specs=[VMEM] * len(outs),
        scratch_shapes=[pltpu.VMEM((m, depth), bf16), pltpu.VMEM((m, 128), f32)]
        + [pltpu.VMEM((tm, tn), f32)] * 2,
        compiler_params=params(9 if keep else 12),
        cost_estimate=pl.CostEstimate(flops=512 * m * n, bytes_accessed=512 * (m + n), transcendentals=m * n),
    )(*operands)


def reorder_kernel(tokens, table_ref, arrived_ref, out_ref, norm_ref):
    for p in range(table_ref.shape[0]):
        start = pl.multiple_of(table_ref[p] * tokens, tokens)
        out_ref[p * tokens : (p + 1) * tokens, :] = arrived_ref[pl.ds(start, tokens), :]

    @pl.loop(0, arrived_ref.shape[1] // 128)
    def _(g):
        cols = pl.ds(pl.multiple_of(g * 128, 128), 128)
        norm_ref[:, cols] = jnp.sum(jnp.square(arrived_ref[:, cols].astype(f32)), 0, keepdims=True)


def reorder_call(arrived, table, tokens):
    return pl.pallas_call(
        functools.partial(reorder_kernel, tokens),
        out_shape=[
            jax.ShapeDtypeStruct(arrived.shape, bf16),
            jax.ShapeDtypeStruct((1, arrived.shape[1]), f32),
        ],
        in_specs=[pl.BlockSpec(memory_space=pltpu.SMEM), VMEM],
        out_specs=[VMEM] * 2,
        compiler_params=params(8),
    )(table, arrived)


def weights(tile_max_ref, lse_ref, t):
    return jnp.exp2(KAPPA * tile_max_ref[pl.ds(t, 1), :] - lse_ref[...])


def row_sum_kernel(chained, kept_ref, tile_max_ref, lse_ref, *rest):
    rest = list(rest)
    first = rest.pop(0) if chained else None
    out_ref, wide, partial = rest
    rows_here, cols_here = kept_ref.shape
    tiles = tile_max_ref.shape[0]
    tm = rows_here // tiles
    span, lane_block, height = 1024, 256, 64

    @pl.loop(0, tiles)
    def _(t):
        wide[...] = jnp.broadcast_to(weights(tile_max_ref, lse_ref, t), (16, cols_here)).astype(bf16)

        @pl.loop(0, tm // height)
        def _(g):
            rows = pl.ds(pl.multiple_of(t * tm + g * height, height), height)
            acc = jnp.zeros((height, 128), f32)
            for c in range(0, cols_here, span):
                part = None
                for k in range(c, min(c + span, cols_here), lane_block):
                    w = jnp.concatenate([wide[:, k : k + lane_block]] * (height // 16), 0)
                    term = kept_ref[rows, k : k + lane_block] * w
                    part = term if part is None else part + term
                part = part.astype(f32)
                for k in range(0, lane_block, 128):
                    acc = acc + part[:, k : k + 128]
            partial[rows, :] = acc

    @pl.loop(0, rows_here // 128)
    def _(g):
        rows = pl.ds(pl.multiple_of(g * 128, 128), 128)
        total = jnp.sum(partial[rows, :].T, axis=0, keepdims=True)
        out_ref[:, rows] = first[:, rows] + total if chained else total


def row_sum_call(kept, tile_max, lse, first=None):
    operands = (kept, tile_max, lse) if first is None else (kept, tile_max, lse, first)
    m, n = kept.shape
    return pl.pallas_call(
        functools.partial(row_sum_kernel, first is not None),
        out_shape=jax.ShapeDtypeStruct((1, m), f32),
        in_specs=[VMEM] * len(operands),
        out_specs=VMEM,
        scratch_shapes=[pltpu.VMEM((16, n), bf16), pltpu.VMEM((m, 128), f32)],
        compiler_params=params(3),
        cost_estimate=pl.CostEstimate(flops=2 * m * n, bytes_accessed=2 * m * n, transcendentals=0),
    )(*operands)


def col_sum_kernel(kept_ref, tile_max_ref, lse_ref, row_sum_ref, out_ref, wide):
    rows_here, cols_here = kept_ref.shape
    tiles = tile_max_ref.shape[0]
    tm = rows_here // tiles
    width = 896

    @pl.loop(0, rows_here // 128)
    def _(g):
        rows = pl.ds(pl.multiple_of(g * 128, 128), 128)
        scale = 1.0 / jnp.maximum(row_sum_ref[:, rows], SMALLEST)
        wide[rows, :] = jnp.broadcast_to(scale, (128, 128)).T.astype(bf16)

    least = jnp.min(row_sum_ref[...], axis=1, keepdims=True)
    out_ref[:, cols_here:] = jnp.broadcast_to(jnp.where(least < SMALLEST, 1.0, 0.0), (1, 128))

    @pl.loop(0, cols_here // width)
    def _(n):
        start = pl.multiple_of(n * width, 128)

        def tile(t, total):
            acc = jnp.zeros((16, width), f32)
            for g in range(tm // 64):
                part = None
                for h in range(4):
                    rows = pl.ds(pl.multiple_of(t * tm + g * 64 + h * 16, 16), 16)
                    scale = jnp.concatenate([wide[rows, :]] * (width // 128), 1)
                    term = kept_ref[rows, pl.ds(start, width)] * scale
                    part = term if part is None else part + term
                acc = acc + part.astype(f32)
            acc = jnp.sum(acc, 0, keepdims=True)
            cols = pl.ds(start, width)
            return total + acc * jnp.exp2(KAPPA * tile_max_ref[pl.ds(t, 1), cols] - lse_ref[:, cols])

        out_ref[:, pl.ds(start, width)] = lax.fori_loop(0, tiles, tile, jnp.zeros((1, width), f32))


def col_sum_call(kept, tile_max, lse, row_sums):
    m, n = kept.shape
    return pl.pallas_call(
        col_sum_kernel,
        out_shape=jax.ShapeDtypeStruct((1, n + 128), f32),
        in_specs=[VMEM] * 4,
        out_specs=VMEM,
        scratch_shapes=[pltpu.VMEM((m, 128), bf16)],
        compiler_params=params(3),
        cost_estimate=pl.CostEstimate(flops=2 * m * n, bytes_accessed=2 * m * n, transcendentals=0),
    )(kept, tile_max, lse, row_sums)


def group_steps(axis, size):
    step = 1
    while step < size:
        yield lambda x, s=step: lax.ppermute(x, axis, [(i, i ^ s) for i in range(size)])
        step *= 2


def merge_kernel(last, mine_ref, other_ref, out_ref):
    mine, other = mine_ref[...], other_ref[...]
    top = jnp.maximum(mine[:1], other[:1])
    total = mine[1:] * jnp.exp2((mine[:1] - top) * KAPPA) + other[1:] * jnp.exp2((other[:1] - top) * KAPPA)
    if last:
        out_ref[...] = KAPPA * top + jnp.log2(total)
    else:
        out_ref[0:1, :] = top
        out_ref[1:2, :] = total


def add_kernel(mine_ref, other_ref, out_ref):
    out_ref[...] = mine_ref[...] + other_ref[...]


def small_call(kernel, shape, *operands):
    return pl.pallas_call(
        kernel,
        out_shape=jax.ShapeDtypeStruct(shape, f32),
        in_specs=[VMEM] * len(operands),
        out_specs=VMEM,
        compiler_params=params(1),
    )(*operands)


def group_lse(pair, exchange_steps):
    exchange_steps = list(exchange_steps)
    for k, exchange in enumerate(exchange_steps):
        last = k + 1 == len(exchange_steps)
        shape = (1 if last else 2, pair.shape[1])
        pair = small_call(functools.partial(merge_kernel, last), shape, pair, exchange(pair))
    return pair


def group_sum(x, exchange_steps):
    for exchange in exchange_steps:
        x = small_call(add_kernel, x.shape, x, exchange(x))
    return x


def swap(x, axis, size, mask):
    return lax.ppermute(x, axis, [(i, i ^ mask) for i in range(size)])


def gather_order(size, near):
    far = size // near
    return [f * near + k for k in range(near) for f in range(far)]


def after(x, other):
    return lax.optimization_barrier((x, other))[0]


CHUNKS = 4
HALVES = 2


def per_device(aa_size, ba_size, acts_a, acts_b):
    def over_a():
        return group_steps("aa", aa_size)

    def over_b():
        return group_steps("ba", ba_size)

    cols_here = acts_b.shape[1]
    width = cols_here // CHUNKS
    half = cols_here // HALVES
    near = aa_size // 4
    far_masks = [f * near for f in range(1, 4)]

    tokens = acts_b.shape[0]
    per_block = aa_size // ba_size
    arrival = gather_order(ba_size, 2)
    place = jnp.array([arrival.index(v) for v in range(ba_size)], jnp.int32)
    token_block = lax.axis_index("aa") ^ jnp.array(gather_order(aa_size, near), jnp.int32)
    table = place[(token_block // per_block) ^ lax.axis_index("ba")] * per_block + token_block % per_block
    group = [acts_a] + [swap(acts_a, "ba", ba_size, mask) for mask in range(2, ba_size, 2)]
    far_a = jnp.concatenate(group, 0)
    arrived_a = jnp.concatenate([far_a, swap(far_a, "ba", ba_size, 1)], 0)
    whole_a, norm_a = reorder_call(arrived_a, table, tokens)

    chunks, norms_b, states, sides = [], [], [], []

    def start_chunk(c):
        own = acts_b[:, c * width : (c + 1) * width]
        if c:
            own = after(own, sides[c - 1] if c >= 2 else far_a)
        group = [own] + [swap(own, "aa", aa_size, mask) for mask in far_masks]
        group[-1] = after(group[-1], states[c - 2] if c >= 2 else far_a)
        mine = jnp.concatenate(group, 0)
        sides.append(mine)
        return [mine] + [swap(mine, "aa", aa_size, k) for k in range(1, near)]

    coming = start_chunk(0)
    for c in range(CHUNKS):
        group = coming
        group[-1] = after(group[-1], states[c - 1] if c else whole_a)
        chunk = jnp.concatenate(group, 0)
        chunks.append(chunk)
        if c + 1 < CHUNKS:
            coming = start_chunk(c + 1)
            chunk = after(chunk, sides[c + 1])
        state, norm = lse_call(chunk, whole_a, None, states[c - 1] if c else None)
        states.append(state)
        norms_b.append(norm)
    row_lse = group_lse(states[-1], over_b())
    per_half = CHUNKS // HALVES
    halves = [jnp.concatenate(chunks[h * per_half : (h + 1) * per_half], 1) for h in range(HALVES)]
    log_n = math.log(NA)

    def potential_a_of(row_lse):
        return -epsilon * (log_n + LN2 * (row_lse - (0.5 * KAPPA) * norm_a))

    def potential_b_of(col_lse, norm_b):
        return -epsilon * LN2 * (col_lse - (0.5 * KAPPA) * norm_b)

    row_bias, halves = lax.optimization_barrier((row_lse * (-1.0 / KAPPA), halves))
    col_lse, tile_max, kept = [], [], []
    for part in halves:
        state, top, p = lse_call(whole_a, part, row_bias, keep=True)
        col_lse.append(group_lse(state, over_a()))
        tile_max.append(top)
        kept.append(pltpu.with_memory_space_constraint(p, pltpu.VMEM))
    row_sums = None
    for h in range(HALVES):
        row_sums = row_sum_call(kept[h], tile_max[h], col_lse[h], row_sums)
    row_sums = group_sum(row_sums, over_b())
    col_sums = []
    for h in range(HALVES):
        sums = col_sum_call(kept[h], tile_max[h], col_lse[h], row_sums)
        col_sums.append(group_sum(sums, over_a()))

    def half_norms(h):
        return jnp.concatenate(norms_b[h * per_half : (h + 1) * per_half], 1)

    def quick(_):
        second_a = potential_a_of(row_lse) - epsilon * jnp.log(row_sums)
        second_b = [
            potential_b_of(col_lse[h], half_norms(h)) - epsilon * jnp.log(col_sums[h][:, :half])
            for h in range(HALVES)
        ]
        return second_a, jnp.concatenate(second_b, 1)

    def exact(_):
        state = None
        for part, lse in zip(halves, col_lse):
            (state,) = lse_call(part, whole_a, lse * (-1.0 / KAPPA), state)
        again = group_lse(state, over_b())
        second_b = []
        for h, part in enumerate(halves):
            (state,) = lse_call(whole_a, part, again * (-1.0 / KAPPA))
            second_b.append(potential_b_of(group_lse(state, over_a()), half_norms(h)))
        return potential_a_of(again), jnp.concatenate(second_b, 1)

    second_a, second_b = lax.cond(col_sums[-1][0, half] > 0.0, exact, quick, 0)
    return second_a.reshape(-1), second_b.reshape(-1)


def solution(mesh):
    in_specs = (P("ba", "aa"), P("aa", "ba"))
    out_specs = (P("aa"), P("ba"))
    return jax.shard_map(
        functools.partial(per_device, mesh.shape["aa"], mesh.shape["ba"]),
        mesh=mesh, in_specs=in_specs, out_specs=out_specs, check_vma=False,
    )
```

```python
import functools
import math

import jax
import jax.numpy as jnp
from jax import lax
from jax.experimental import pallas as pl
from jax.experimental.pallas import tpu as pltpu
from jax.sharding import PartitionSpec as P

NA = 28672
NB = 28672
TOKENS = 256
epsilon = 0.01

f32 = jnp.float32
bf16 = jnp.bfloat16
VMEM = pl.BlockSpec(memory_space=pltpu.VMEM)

KAPPA = math.log2(math.e) * 2.0 / (TOKENS * epsilon)
LN2 = math.log(2.0)
SMALLEST = 2.0**-60


def params(mib):
    return pltpu.CompilerParams(vmem_limit_bytes=mib << 20)


def lse_kernel(tm, tn, biased, chained, keep, lhs_ref, rhs_ref, *rest):
    rest = list(rest)
    bias_ref = rest.pop(0) if biased else None
    state_in = rest.pop(0) if chained else None
    state_ref = rest.pop(0)
    norm_ref = None if biased else rest.pop(0)
    if keep:
        tile_max_ref, kept_ref = rest.pop(0), rest.pop(0)
    turned, wide, *blocks = rest
    row_tiles = lhs_ref.shape[1] // tm
    total = row_tiles * (rhs_ref.shape[1] // tn)
    sub = 64 if keep or tm % 128 else 128
    lanes = tn // 128

    @pl.loop(0, lhs_ref.shape[1] // 128)
    def _(g):
        rows = pl.ds(pl.multiple_of(g * 128, 128), 128)
        turned[rows, :] = lhs_ref[:, rows].T
        if biased:
            bias = bias_ref[:, rows]
        else:
            norm = jnp.sum(jnp.square(lhs_ref[:, rows].astype(f32)), 0, keepdims=True)
            norm_ref[:, rows] = norm
            bias = -0.5 * norm
        wide[rows, :] = jnp.broadcast_to(bias, (128, 128)).T

    def cols(n):
        return pl.ds(pl.multiple_of(n * tn, tn), tn)

    def product(n, t, block):
        rows = pl.ds(pl.multiple_of(t * tm, tm), tm)
        block[...] = jnp.dot(turned[rows, :], rhs_ref[:, cols(n)], preferred_element_type=f32)

    def scores(t, k, block):
        rows = pl.ds(pl.multiple_of(t * tm + k, 64), sub)
        return block[k : k + sub, :] + jnp.concatenate([wide[rows, :]] * lanes, 1)

    def raised(n, t, block, upper, total_sum):
        new = upper
        for k in range(0, tm, sub):
            x = scores(t, k, block)
            if keep:
                block[k : k + sub, :] = x
            new = jnp.maximum(new, x.reshape(sub // 8, 8, tn).max(0))
        row = new.max(0, keepdims=True)
        new = jnp.broadcast_to(row, (8, tn))
        return row, new, total_sum * jnp.exp2((upper - new) * KAPPA)

    def reduce_kept(n, t, block, upper, total_sum):
        row, new, total_sum = raised(n, t, block, upper, total_sum)
        for k in range(0, tm, sub):
            rows = pl.ds(pl.multiple_of(t * tm + k, 64), sub)
            p = jnp.exp2((block[k : k + sub, :] - row) * KAPPA)
            total_sum = total_sum + p.reshape(sub // 8, 8, tn).sum(0)
            kept_ref[rows, cols(n)] = p.astype(bf16)
        tile_max_ref[pl.ds(t, 1), cols(n)] = row
        return new, total_sum

    def reduce_only(n, t, block, upper, total_sum):
        row, new, total_sum = raised(n, t, block, upper, total_sum)
        for k in range(0, tm, sub):
            p = jnp.exp2(((scores(t, k, block) - row) * KAPPA).astype(bf16))
            for g in range(0, sub, 64):
                part = (p[g : g + 16] + p[g + 16 : g + 32]) + (p[g + 32 : g + 48] + p[g + 48 : g + 64])
                part = part.astype(f32)
                total_sum = total_sum + (part[:8] + part[8:])
        return new, total_sum

    reduce = reduce_kept if keep else reduce_only
    product(0, 0, blocks[0])
    first_sublane = lax.broadcasted_iota(jnp.int32, (8, tn), 0) == 0

    def pair(k, carry):
        upper, total_sum = carry
        for half in range(2):
            step = 2 * k + half
            n = step // row_tiles
            t = step - n * row_tiles
            after = jnp.minimum(step + 1, total - 1)
            n_after = after // row_tiles
            if chained:
                start = state_in[:, cols(n)]
                start_max = jnp.broadcast_to(start[:1], (8, tn))
                start_sum = jnp.where(first_sublane, jnp.broadcast_to(start[1:], (8, tn)), 0.0)
            else:
                start_max, start_sum = jnp.full((8, tn), -1e30, f32), jnp.zeros((8, tn), f32)
            upper = jnp.where(t == 0, start_max, upper)
            total_sum = jnp.where(t == 0, start_sum, total_sum)
            product(n_after, after - n_after * row_tiles, blocks[1 - half])
            upper, total_sum = reduce(n, t, blocks[half], upper, total_sum)
            state_ref[0:1, cols(n)] = upper[:1]
            state_ref[1:2, cols(n)] = jnp.sum(total_sum, 0, keepdims=True)
        return upper, total_sum

    zeros = jnp.zeros((8, tn), f32)
    lax.fori_loop(0, total // 2, pair, (zeros, zeros))


def lse_call(lhs, rhs, bias=None, state=None, keep=False):
    depth, m = lhs.shape
    n = rhs.shape[1]
    tm, tn = (896, 512) if n % 512 == 0 else (448, 896)
    outs = [jax.ShapeDtypeStruct((2, n), f32)]
    operands = [lhs, rhs]
    if bias is None:
        outs += [jax.ShapeDtypeStruct((1, m), f32)]
    else:
        operands += [bias]
    if state is not None:
        operands += [state]
    if keep:
        outs += [jax.ShapeDtypeStruct((m // tm, n), f32), pltpu.VMEM((m, n), bf16)]
    return pl.pallas_call(
        functools.partial(lse_kernel, tm, tn, bias is not None, state is not None, keep),
        out_shape=outs,
        in_specs=[VMEM] * len(operands),
        out_specs=[VMEM] * len(outs),
        scratch_shapes=[pltpu.VMEM((m, depth), bf16), pltpu.VMEM((m, 128), f32)]
        + [pltpu.VMEM((tm, tn), f32)] * 2,
        compiler_params=params(9 if keep else 12),
        cost_estimate=pl.CostEstimate(flops=512 * m * n, bytes_accessed=512 * (m + n), transcendentals=m * n),
    )(*operands)


def reorder_kernel(tokens, table_ref, arrived_ref, out_ref, norm_ref):
    for p in range(table_ref.shape[0]):
        start = pl.multiple_of(table_ref[p] * tokens, tokens)
        out_ref[p * tokens : (p + 1) * tokens, :] = arrived_ref[pl.ds(start, tokens), :]

    @pl.loop(0, arrived_ref.shape[1] // 128)
    def _(g):
        cols = pl.ds(pl.multiple_of(g * 128, 128), 128)
        norm_ref[:, cols] = jnp.sum(jnp.square(arrived_ref[:, cols].astype(f32)), 0, keepdims=True)


def reorder_call(arrived, table, tokens):
    return pl.pallas_call(
        functools.partial(reorder_kernel, tokens),
        out_shape=[
            jax.ShapeDtypeStruct(arrived.shape, bf16),
            jax.ShapeDtypeStruct((1, arrived.shape[1]), f32),
        ],
        in_specs=[pl.BlockSpec(memory_space=pltpu.SMEM), VMEM],
        out_specs=[VMEM] * 2,
        compiler_params=params(8),
    )(table, arrived)


def weights(tile_max_ref, lse_ref, t):
    return jnp.exp2(KAPPA * tile_max_ref[pl.ds(t, 1), :] - lse_ref[...])


def row_sum_kernel(chained, kept_ref, tile_max_ref, lse_ref, *rest):
    rest = list(rest)
    first = rest.pop(0) if chained else None
    out_ref, wide, partial = rest
    rows_here, cols_here = kept_ref.shape
    tiles = tile_max_ref.shape[0]
    tm = rows_here // tiles
    span, lane_block, height = 1024, 256, 64

    @pl.loop(0, tiles)
    def _(t):
        wide[...] = jnp.broadcast_to(weights(tile_max_ref, lse_ref, t), (16, cols_here)).astype(bf16)

        @pl.loop(0, tm // height)
        def _(g):
            rows = pl.ds(pl.multiple_of(t * tm + g * height, height), height)
            acc = jnp.zeros((height, 128), f32)
            for c in range(0, cols_here, span):
                part = None
                for k in range(c, min(c + span, cols_here), lane_block):
                    w = jnp.concatenate([wide[:, k : k + lane_block]] * (height // 16), 0)
                    term = kept_ref[rows, k : k + lane_block] * w
                    part = term if part is None else part + term
                part = part.astype(f32)
                for k in range(0, lane_block, 128):
                    acc = acc + part[:, k : k + 128]
            partial[rows, :] = acc

    @pl.loop(0, rows_here // 128)
    def _(g):
        rows = pl.ds(pl.multiple_of(g * 128, 128), 128)
        total = jnp.sum(partial[rows, :].T, axis=0, keepdims=True)
        out_ref[:, rows] = first[:, rows] + total if chained else total


def row_sum_call(kept, tile_max, lse, first=None):
    operands = (kept, tile_max, lse) if first is None else (kept, tile_max, lse, first)
    m, n = kept.shape
    return pl.pallas_call(
        functools.partial(row_sum_kernel, first is not None),
        out_shape=jax.ShapeDtypeStruct((1, m), f32),
        in_specs=[VMEM] * len(operands),
        out_specs=VMEM,
        scratch_shapes=[pltpu.VMEM((16, n), bf16), pltpu.VMEM((m, 128), f32)],
        compiler_params=params(3),
        cost_estimate=pl.CostEstimate(flops=2 * m * n, bytes_accessed=2 * m * n, transcendentals=0),
    )(*operands)


def col_sum_kernel(kept_ref, tile_max_ref, lse_ref, row_sum_ref, out_ref, wide):
    rows_here, cols_here = kept_ref.shape
    tiles = tile_max_ref.shape[0]
    tm = rows_here // tiles
    width = 896

    @pl.loop(0, rows_here // 128)
    def _(g):
        rows = pl.ds(pl.multiple_of(g * 128, 128), 128)
        scale = 1.0 / jnp.maximum(row_sum_ref[:, rows], SMALLEST)
        wide[rows, :] = jnp.broadcast_to(scale, (128, 128)).T.astype(bf16)

    least = jnp.min(row_sum_ref[...], axis=1, keepdims=True)
    out_ref[:, cols_here:] = jnp.broadcast_to(jnp.where(least < SMALLEST, 1.0, 0.0), (1, 128))

    @pl.loop(0, cols_here // width)
    def _(n):
        start = pl.multiple_of(n * width, 128)

        def tile(t, total):
            acc = jnp.zeros((16, width), f32)
            for g in range(tm // 64):
                part = None
                for h in range(4):
                    rows = pl.ds(pl.multiple_of(t * tm + g * 64 + h * 16, 16), 16)
                    scale = jnp.concatenate([wide[rows, :]] * (width // 128), 1)
                    term = kept_ref[rows, pl.ds(start, width)] * scale
                    part = term if part is None else part + term
                acc = acc + part.astype(f32)
            acc = jnp.sum(acc, 0, keepdims=True)
            cols = pl.ds(start, width)
            return total + acc * jnp.exp2(KAPPA * tile_max_ref[pl.ds(t, 1), cols] - lse_ref[:, cols])

        out_ref[:, pl.ds(start, width)] = lax.fori_loop(0, tiles, tile, jnp.zeros((1, width), f32))


def col_sum_call(kept, tile_max, lse, row_sums):
    m, n = kept.shape
    return pl.pallas_call(
        col_sum_kernel,
        out_shape=jax.ShapeDtypeStruct((1, n + 128), f32),
        in_specs=[VMEM] * 4,
        out_specs=VMEM,
        scratch_shapes=[pltpu.VMEM((m, 128), bf16)],
        compiler_params=params(3),
        cost_estimate=pl.CostEstimate(flops=2 * m * n, bytes_accessed=2 * m * n, transcendentals=0),
    )(kept, tile_max, lse, row_sums)


def near_first(near):
    return [[1 << k] for k in range(near.bit_length() - 1)] + [[near, 2 * near, 3 * near]]


def pairwise(size):
    return [[1 << k] for k in range(size.bit_length() - 1)]


def add_in_pairs(values):
    while len(values) > 1:
        values = [values[k] + values[k + 1] for k in range(0, len(values), 2)]
    return values[0]


def merge_kernel(last, *refs):
    *in_refs, out_ref = refs
    pairs = [ref[...] for ref in in_refs]
    top = functools.reduce(jnp.maximum, [pair[:1] for pair in pairs])
    total = add_in_pairs([pair[1:] * jnp.exp2((pair[:1] - top) * KAPPA) for pair in pairs])
    if last:
        out_ref[...] = KAPPA * top + jnp.log2(total)
    else:
        out_ref[0:1, :] = top
        out_ref[1:2, :] = total


def add_kernel(*refs):
    *in_refs, out_ref = refs
    out_ref[...] = add_in_pairs([ref[...] for ref in in_refs])


def small_call(kernel, shape, *operands):
    return pl.pallas_call(
        kernel,
        out_shape=jax.ShapeDtypeStruct(shape, f32),
        in_specs=[VMEM] * len(operands),
        out_specs=VMEM,
        compiler_params=params(1),
    )(*operands)


def swap(x, axis, size, mask):
    return lax.ppermute(x, axis, [(i, i ^ mask) for i in range(size)])


def group_lse(pair, axis, size, steps):
    for k, masks in enumerate(steps):
        last = k + 1 == len(steps)
        shape = (1 if last else 2, pair.shape[1])
        others = [swap(pair, axis, size, mask) for mask in masks]
        pair = small_call(functools.partial(merge_kernel, last), shape, pair, *others)
    return pair


def group_sum(x, axis, size, steps):
    for masks in steps:
        x = small_call(add_kernel, x.shape, x, *[swap(x, axis, size, mask) for mask in masks])
    return x


def gather_order(size, near):
    far = size // near
    return [f * near + k for k in range(near) for f in range(far)]


def after(x, other):
    return lax.optimization_barrier((x, other))[0]


CHUNKS = 4
HALVES = 2


def per_device(aa_size, ba_size, acts_a, acts_b):
    cols_here = acts_b.shape[1]
    width = cols_here // CHUNKS
    half = cols_here // HALVES
    near = aa_size // 4
    far_masks = [f * near for f in range(1, 4)]
    over_a = ("aa", aa_size, near_first(near))
    over_b = ("ba", ba_size, pairwise(ba_size))

    tokens = acts_b.shape[0]
    per_block = aa_size // ba_size
    arrival = gather_order(ba_size, 2)
    place = jnp.array([arrival.index(v) for v in range(ba_size)], jnp.int32)
    token_block = lax.axis_index("aa") ^ jnp.array(gather_order(aa_size, near), jnp.int32)
    table = place[(token_block // per_block) ^ lax.axis_index("ba")] * per_block + token_block % per_block
    group = [acts_a] + [swap(acts_a, "ba", ba_size, mask) for mask in range(2, ba_size, 2)]
    far_a = jnp.concatenate(group, 0)
    arrived_a = jnp.concatenate([far_a, swap(far_a, "ba", ba_size, 1)], 0)
    whole_a, norm_a = reorder_call(arrived_a, table, tokens)

    chunks, norms_b, states, sides = [], [], [], []

    def start_chunk(c):
        own = acts_b[:, c * width : (c + 1) * width]
        if c:
            own = after(own, sides[c - 1] if c >= 2 else far_a)
        group = [own] + [swap(own, "aa", aa_size, mask) for mask in far_masks]
        first = states[c - 2] if c >= 2 else far_a
        group = [own] + [after(piece, first) for piece in group[1:]]
        mine = jnp.concatenate(group, 0)
        sides.append(mine)
        return [mine] + [swap(mine, "aa", aa_size, k) for k in range(1, near)]

    coming = start_chunk(0)
    for c in range(CHUNKS):
        group = coming
        first = states[c - 1] if c else whole_a
        group = group[:1] + [after(piece, first) for piece in group[1:]]
        chunk = jnp.concatenate(group, 0)
        chunks.append(chunk)
        if c + 1 < CHUNKS:
            coming = start_chunk(c + 1)
            chunk = after(chunk, sides[c + 1])
        state, norm = lse_call(chunk, whole_a, None, states[c - 1] if c else None)
        states.append(state)
        norms_b.append(norm)
    row_lse = group_lse(states[-1], *over_b)
    per_half = CHUNKS // HALVES
    halves = [jnp.concatenate(chunks[h * per_half : (h + 1) * per_half], 1) for h in range(HALVES)]
    log_n = math.log(NA)

    def potential_a_of(row_lse):
        return -epsilon * (log_n + LN2 * (row_lse - (0.5 * KAPPA) * norm_a))

    def potential_b_of(col_lse, norm_b):
        return -epsilon * LN2 * (col_lse - (0.5 * KAPPA) * norm_b)

    row_bias, halves = lax.optimization_barrier((row_lse * (-1.0 / KAPPA), halves))
    col_lse, tile_max, kept = [], [], []
    for part in halves:
        state, top, p = lse_call(whole_a, part, row_bias, keep=True)
        col_lse.append(group_lse(state, *over_a))
        tile_max.append(top)
        kept.append(pltpu.with_memory_space_constraint(p, pltpu.VMEM))
    row_sums = None
    for h in range(HALVES):
        row_sums = row_sum_call(kept[h], tile_max[h], col_lse[h], row_sums)
    row_sums = group_sum(row_sums, *over_b)
    col_sums = []
    for h in range(HALVES):
        sums = col_sum_call(kept[h], tile_max[h], col_lse[h], row_sums)
        col_sums.append(group_sum(sums, *over_a))

    def half_norms(h):
        return jnp.concatenate(norms_b[h * per_half : (h + 1) * per_half], 1)

    def quick(_):
        second_a = potential_a_of(row_lse) - epsilon * jnp.log(row_sums)
        second_b = [
            potential_b_of(col_lse[h], half_norms(h)) - epsilon * jnp.log(col_sums[h][:, :half])
            for h in range(HALVES)
        ]
        return second_a, jnp.concatenate(second_b, 1)

    def exact(_):
        state = None
        for part, lse in zip(halves, col_lse):
            (state,) = lse_call(part, whole_a, lse * (-1.0 / KAPPA), state)
        again = group_lse(state, *over_b)
        second_b = []
        for h, part in enumerate(halves):
            (state,) = lse_call(whole_a, part, again * (-1.0 / KAPPA))
            second_b.append(potential_b_of(group_lse(state, *over_a), half_norms(h)))
        return potential_a_of(again), jnp.concatenate(second_b, 1)

    second_a, second_b = lax.cond(col_sums[-1][0, half] > 0.0, exact, quick, 0)
    return second_a.reshape(-1), second_b.reshape(-1)


def solution(mesh):
    in_specs = (P("ba", "aa"), P("aa", "ba"))
    out_specs = (P("aa"), P("ba"))
    return jax.shard_map(
        functools.partial(per_device, mesh.shape["aa"], mesh.shape["ba"]),
        mesh=mesh, in_specs=in_specs, out_specs=out_specs, check_vma=False,
    )
```

```python
import functools
import math

import jax
import jax.numpy as jnp
from jax import lax
from jax.experimental import pallas as pl
from jax.experimental.pallas import tpu as pltpu
from jax.sharding import PartitionSpec as P

NA = 28672
NB = 28672
TOKENS = 256
epsilon = 0.01

f32 = jnp.float32
bf16 = jnp.bfloat16
VMEM = pl.BlockSpec(memory_space=pltpu.VMEM)

KAPPA = math.log2(math.e) * 2.0 / (TOKENS * epsilon)
LN2 = math.log(2.0)
SMALLEST = 2.0**-60


def params(mib):
    return pltpu.CompilerParams(vmem_limit_bytes=mib << 20)


def lse_kernel(tm, tn, biased, chained, keep, staged, lhs_ref, rhs_ref, *rest):
    rest = list(rest)
    bias_ref = rest.pop(0) if biased else None
    state_in = rest.pop(0) if chained else None
    state_ref = rest.pop(0)
    norm_ref = None if biased else rest.pop(0)
    if keep:
        tile_max_ref, kept_ref = rest.pop(0), rest.pop(0)
    turned, wide, *blocks = rest
    if staged:
        sent = blocks.pop()
        stage = blocks.pop()
    row_tiles = lhs_ref.shape[1] // tm
    total = row_tiles * (rhs_ref.shape[1] // tn)
    sub = 64 if keep or tm % 128 else 128
    lanes = tn // 128

    @pl.loop(0, lhs_ref.shape[1] // 128)
    def _(g):
        rows = pl.ds(pl.multiple_of(g * 128, 128), 128)
        turned[rows, :] = lhs_ref[:, rows].T
        if biased:
            bias = bias_ref[:, rows]
        else:
            norm = jnp.sum(jnp.square(lhs_ref[:, rows].astype(f32)), 0, keepdims=True)
            norm_ref[:, rows] = norm
            bias = -0.5 * norm
        wide[rows, :] = jnp.broadcast_to(bias, (128, 128)).T

    def cols(n):
        return pl.ds(pl.multiple_of(n * tn, tn), tn)

    def product(n, t, block):
        rows = pl.ds(pl.multiple_of(t * tm, tm), tm)
        block[...] = jnp.dot(turned[rows, :], rhs_ref[:, cols(n)], preferred_element_type=f32)

    def scores(t, k, block):
        rows = pl.ds(pl.multiple_of(t * tm + k, 64), sub)
        return block[k : k + sub, :] + jnp.concatenate([wide[rows, :]] * lanes, 1)

    def raised(n, t, block, upper, total_sum):
        new = upper
        for k in range(0, tm, sub):
            x = scores(t, k, block)
            if keep:
                block[k : k + sub, :] = x
            new = jnp.maximum(new, x.reshape(sub // 8, 8, tn).max(0))
        row = new.max(0, keepdims=True)
        new = jnp.broadcast_to(row, (8, tn))
        return row, new, total_sum * jnp.exp2((upper - new) * KAPPA)

    def send(step, parity, half):
        n = step // row_tiles
        rows = pl.ds(pl.multiple_of((step - n * row_tiles) * tm, tm), tm)
        return pltpu.make_async_copy(
            stage.at[parity, half], kept_ref.at[rows, cols(n)], sent.at[parity, half]
        )

    def reduce_kept(n, t, block, upper, total_sum, slot):
        row, new, total_sum = raised(n, t, block, upper, total_sum)
        for k in range(0, tm, sub):
            rows = pl.ds(pl.multiple_of(t * tm + k, 64), sub)
            p = jnp.exp2((block[k : k + sub, :] - row) * KAPPA)
            total_sum = total_sum + p.reshape(sub // 8, 8, tn).sum(0)
            if staged:
                stage[slot[0], slot[1], k : k + sub, :] = p.astype(bf16)
            else:
                kept_ref[rows, cols(n)] = p.astype(bf16)
        tile_max_ref[pl.ds(t, 1), cols(n)] = row
        return new, total_sum

    def reduce_only(n, t, block, upper, total_sum, slot):
        row, new, total_sum = raised(n, t, block, upper, total_sum)
        for k in range(0, tm, sub):
            p = jnp.exp2(((scores(t, k, block) - row) * KAPPA).astype(bf16))
            for g in range(0, sub, 64):
                part = (p[g : g + 16] + p[g + 16 : g + 32]) + (p[g + 32 : g + 48] + p[g + 48 : g + 64])
                part = part.astype(f32)
                total_sum = total_sum + (part[:8] + part[8:])
        return new, total_sum

    reduce = reduce_kept if keep else reduce_only
    product(0, 0, blocks[0])
    first_sublane = lax.broadcasted_iota(jnp.int32, (8, tn), 0) == 0

    def pair(k, carry):
        upper, total_sum = carry
        if staged:
            @pl.when(k >= 2)
            def _():
                for half in range(2):
                    send(2 * k + half, k % 2, half).wait()

        for half in range(2):
            step = 2 * k + half
            n = step // row_tiles
            t = step - n * row_tiles
            after = jnp.minimum(step + 1, total - 1)
            n_after = after // row_tiles
            if chained:
                start = state_in[:, cols(n)]
                start_max = jnp.broadcast_to(start[:1], (8, tn))
                start_sum = jnp.where(first_sublane, jnp.broadcast_to(start[1:], (8, tn)), 0.0)
            else:
                start_max, start_sum = jnp.full((8, tn), -1e30, f32), jnp.zeros((8, tn), f32)
            upper = jnp.where(t == 0, start_max, upper)
            total_sum = jnp.where(t == 0, start_sum, total_sum)
            product(n_after, after - n_after * row_tiles, blocks[1 - half])
            upper, total_sum = reduce(n, t, blocks[half], upper, total_sum, (k % 2, half))
            state_ref[0:1, cols(n)] = upper[:1]
            state_ref[1:2, cols(n)] = jnp.sum(total_sum, 0, keepdims=True)
        if staged:
            for half in range(2):
                send(2 * k + half, k % 2, half).start()
        return upper, total_sum

    zeros = jnp.zeros((8, tn), f32)
    lax.fori_loop(0, total // 2, pair, (zeros, zeros))
    if staged:
        for step in range(4):
            send(step, step // 2, step % 2).wait()


def lse_call(lhs, rhs, bias=None, state=None, keep=False, staged=False):
    depth, m = lhs.shape
    n = rhs.shape[1]
    tm, tn = (896, 512) if n % 512 == 0 else (448, 896)
    outs = [jax.ShapeDtypeStruct((2, n), f32)]
    operands = [lhs, rhs]
    if bias is None:
        outs += [jax.ShapeDtypeStruct((1, m), f32)]
    else:
        operands += [bias]
    if state is not None:
        operands += [state]
    if keep:
        place = pltpu.HBM if staged else pltpu.VMEM
        outs += [jax.ShapeDtypeStruct((m // tm, n), f32), place((m, n), bf16)]
    return pl.pallas_call(
        functools.partial(lse_kernel, tm, tn, bias is not None, state is not None, keep, staged),
        out_shape=outs,
        in_specs=[VMEM] * len(operands),
        out_specs=[VMEM] * (len(outs) - 1) + [pl.BlockSpec(memory_space=pltpu.HBM) if staged else VMEM],
        scratch_shapes=[pltpu.VMEM((m, depth), bf16), pltpu.VMEM((m, 128), f32)]
        + [pltpu.VMEM((tm, tn), f32)] * 2
        + ([pltpu.VMEM((2, 2, tm, tn), bf16), pltpu.SemaphoreType.DMA((2, 2))] if staged else []),
        compiler_params=params(14 if staged else 9 if keep else 12),
        cost_estimate=pl.CostEstimate(flops=512 * m * n, bytes_accessed=512 * (m + n), transcendentals=m * n),
    )(*operands)


def reorder_kernel(tokens, table_ref, arrived_ref, out_ref, norm_ref):
    for p in range(table_ref.shape[0]):
        start = pl.multiple_of(table_ref[p] * tokens, tokens)
        out_ref[p * tokens : (p + 1) * tokens, :] = arrived_ref[pl.ds(start, tokens), :]

    @pl.loop(0, arrived_ref.shape[1] // 128)
    def _(g):
        cols = pl.ds(pl.multiple_of(g * 128, 128), 128)
        norm_ref[:, cols] = jnp.sum(jnp.square(arrived_ref[:, cols].astype(f32)), 0, keepdims=True)


def reorder_call(arrived, table, tokens):
    return pl.pallas_call(
        functools.partial(reorder_kernel, tokens),
        out_shape=[
            jax.ShapeDtypeStruct(arrived.shape, bf16),
            jax.ShapeDtypeStruct((1, arrived.shape[1]), f32),
        ],
        in_specs=[pl.BlockSpec(memory_space=pltpu.SMEM), VMEM],
        out_specs=[VMEM] * 2,
        compiler_params=params(8),
    )(table, arrived)


def weights(tile_max_ref, lse_ref, t):
    return jnp.exp2(KAPPA * tile_max_ref[pl.ds(t, 1), :] - lse_ref[...])


def row_sum_kernel(chained, kept_ref, tile_max_ref, lse_ref, *rest):
    rest = list(rest)
    first = rest.pop(0) if chained else None
    out_ref, wide, partial = rest
    rows_here, cols_here = kept_ref.shape
    tiles = tile_max_ref.shape[0]
    tm = rows_here // tiles
    span, lane_block, height = 1024, 256, 64

    @pl.loop(0, tiles)
    def _(t):
        wide[...] = jnp.broadcast_to(weights(tile_max_ref, lse_ref, t), (16, cols_here)).astype(bf16)

        @pl.loop(0, tm // height)
        def _(g):
            rows = pl.ds(pl.multiple_of(t * tm + g * height, height), height)
            acc = jnp.zeros((height, 128), f32)
            for c in range(0, cols_here, span):
                part = None
                for k in range(c, min(c + span, cols_here), lane_block):
                    w = jnp.concatenate([wide[:, k : k + lane_block]] * (height // 16), 0)
                    term = kept_ref[rows, k : k + lane_block] * w
                    part = term if part is None else part + term
                part = part.astype(f32)
                for k in range(0, lane_block, 128):
                    acc = acc + part[:, k : k + 128]
            partial[rows, :] = acc

    @pl.loop(0, rows_here // 128)
    def _(g):
        rows = pl.ds(pl.multiple_of(g * 128, 128), 128)
        total = jnp.sum(partial[rows, :].T, axis=0, keepdims=True)
        out_ref[:, rows] = first[:, rows] + total if chained else total


def row_sum_call(kept, tile_max, lse, first=None):
    operands = (kept, tile_max, lse) if first is None else (kept, tile_max, lse, first)
    m, n = kept.shape
    return pl.pallas_call(
        functools.partial(row_sum_kernel, first is not None),
        out_shape=jax.ShapeDtypeStruct((1, m), f32),
        in_specs=[VMEM] * len(operands),
        out_specs=VMEM,
        scratch_shapes=[pltpu.VMEM((16, n), bf16), pltpu.VMEM((m, 128), f32)],
        compiler_params=params(3),
        cost_estimate=pl.CostEstimate(flops=2 * m * n, bytes_accessed=2 * m * n, transcendentals=0),
    )(*operands)


def col_sum_kernel(kept_ref, tile_max_ref, lse_ref, row_sum_ref, out_ref, wide):
    rows_here, cols_here = kept_ref.shape
    tiles = tile_max_ref.shape[0]
    tm = rows_here // tiles
    width = 896

    @pl.loop(0, rows_here // 128)
    def _(g):
        rows = pl.ds(pl.multiple_of(g * 128, 128), 128)
        scale = 1.0 / jnp.maximum(row_sum_ref[:, rows], SMALLEST)
        wide[rows, :] = jnp.broadcast_to(scale, (128, 128)).T.astype(bf16)

    least = jnp.min(row_sum_ref[...], axis=1, keepdims=True)
    out_ref[:, cols_here:] = jnp.broadcast_to(jnp.where(least < SMALLEST, 1.0, 0.0), (1, 128))

    @pl.loop(0, cols_here // width)
    def _(n):
        start = pl.multiple_of(n * width, 128)

        def tile(t, total):
            acc = jnp.zeros((16, width), f32)
            for g in range(tm // 64):
                part = None
                for h in range(4):
                    rows = pl.ds(pl.multiple_of(t * tm + g * 64 + h * 16, 16), 16)
                    scale = jnp.concatenate([wide[rows, :]] * (width // 128), 1)
                    term = kept_ref[rows, pl.ds(start, width)] * scale
                    part = term if part is None else part + term
                acc = acc + part.astype(f32)
            acc = jnp.sum(acc, 0, keepdims=True)
            cols = pl.ds(start, width)
            return total + acc * jnp.exp2(KAPPA * tile_max_ref[pl.ds(t, 1), cols] - lse_ref[:, cols])

        out_ref[:, pl.ds(start, width)] = lax.fori_loop(0, tiles, tile, jnp.zeros((1, width), f32))


def col_sum_call(kept, tile_max, lse, row_sums):
    m, n = kept.shape
    return pl.pallas_call(
        col_sum_kernel,
        out_shape=jax.ShapeDtypeStruct((1, n + 128), f32),
        in_specs=[VMEM] * 4,
        out_specs=VMEM,
        scratch_shapes=[pltpu.VMEM((m, 128), bf16)],
        compiler_params=params(3),
        cost_estimate=pl.CostEstimate(flops=2 * m * n, bytes_accessed=2 * m * n, transcendentals=0),
    )(kept, tile_max, lse, row_sums)


def near_first(near):
    return [[1 << k] for k in range(near.bit_length() - 1)] + [[near, 2 * near, 3 * near]]


def pairwise(size):
    return [[1 << k] for k in range(size.bit_length() - 1)]


def add_in_pairs(values):
    while len(values) > 1:
        values = [values[k] + values[k + 1] for k in range(0, len(values), 2)]
    return values[0]


def merge_kernel(last, *refs):
    *in_refs, out_ref = refs
    pairs = [ref[...] for ref in in_refs]
    top = functools.reduce(jnp.maximum, [pair[:1] for pair in pairs])
    total = add_in_pairs([pair[1:] * jnp.exp2((pair[:1] - top) * KAPPA) for pair in pairs])
    if last:
        out_ref[...] = KAPPA * top + jnp.log2(total)
    else:
        out_ref[0:1, :] = top
        out_ref[1:2, :] = total


def add_kernel(*refs):
    *in_refs, out_ref = refs
    out_ref[...] = add_in_pairs([ref[...] for ref in in_refs])


def small_call(kernel, shape, *operands):
    return pl.pallas_call(
        kernel,
        out_shape=jax.ShapeDtypeStruct(shape, f32),
        in_specs=[VMEM] * len(operands),
        out_specs=VMEM,
        compiler_params=params(1),
    )(*operands)


def swap(x, axis, size, mask):
    return lax.ppermute(x, axis, [(i, i ^ mask) for i in range(size)])


def group_lse(pair, axis, size, steps):
    for k, masks in enumerate(steps):
        last = k + 1 == len(steps)
        shape = (1 if last else 2, pair.shape[1])
        others = [swap(pair, axis, size, mask) for mask in masks]
        pair = small_call(functools.partial(merge_kernel, last), shape, pair, *others)
    return pair


def group_sum(x, axis, size, steps):
    for masks in steps:
        x = small_call(add_kernel, x.shape, x, *[swap(x, axis, size, mask) for mask in masks])
    return x


def gather_order(size, near):
    far = size // near
    return [f * near + k for k in range(near) for f in range(far)]


def after(x, other):
    return lax.optimization_barrier((x, other))[0]


CHUNKS = 4
HALVES = 2


def per_device(aa_size, ba_size, acts_a, acts_b):
    cols_here = acts_b.shape[1]
    width = cols_here // CHUNKS
    half = cols_here // HALVES
    near = aa_size // 4
    far_masks = [f * near for f in range(1, 4)]
    over_a = ("aa", aa_size, near_first(near))
    over_b = ("ba", ba_size, pairwise(ba_size))

    tokens = acts_b.shape[0]
    per_block = aa_size // ba_size
    arrival = gather_order(ba_size, 2)
    place = jnp.array([arrival.index(v) for v in range(ba_size)], jnp.int32)
    token_block = lax.axis_index("aa") ^ jnp.array(gather_order(aa_size, near), jnp.int32)
    table = place[(token_block // per_block) ^ lax.axis_index("ba")] * per_block + token_block % per_block
    group = [acts_a] + [swap(acts_a, "ba", ba_size, mask) for mask in range(2, ba_size, 2)]
    far_a = jnp.concatenate(group, 0)
    arrived_a = jnp.concatenate([far_a, swap(far_a, "ba", ba_size, 1)], 0)
    whole_a, norm_a = reorder_call(arrived_a, table, tokens)

    chunks, norms_b, states, sides = [], [], [], []

    def start_chunk(c):
        own = acts_b[:, c * width : (c + 1) * width]
        if c:
            own = after(own, sides[c - 1] if c >= 2 else far_a)
        group = [own] + [swap(own, "aa", aa_size, mask) for mask in far_masks]
        first = states[c - 2] if c >= 2 else far_a
        group = [own] + [after(piece, first) for piece in group[1:]]
        mine = jnp.concatenate(group, 0)
        sides.append(mine)
        return [mine] + [swap(mine, "aa", aa_size, k) for k in range(1, near)]

    coming = start_chunk(0)
    for c in range(CHUNKS):
        group = coming
        first = states[c - 1] if c else whole_a
        group = group[:1] + [after(piece, first) for piece in group[1:]]
        chunk = jnp.concatenate(group, 0)
        chunks.append(chunk)
        if c + 1 < CHUNKS:
            coming = start_chunk(c + 1)
            chunk = after(chunk, sides[c + 1])
        state, norm = lse_call(chunk, whole_a, None, states[c - 1] if c else None)
        states.append(state)
        norms_b.append(norm)
    row_lse = group_lse(states[-1], *over_b)
    per_half = CHUNKS // HALVES
    halves = [jnp.concatenate(chunks[h * per_half : (h + 1) * per_half], 1) for h in range(HALVES)]
    log_n = math.log(NA)

    def potential_a_of(row_lse):
        return -epsilon * (log_n + LN2 * (row_lse - (0.5 * KAPPA) * norm_a))

    def potential_b_of(col_lse, norm_b):
        return -epsilon * LN2 * (col_lse - (0.5 * KAPPA) * norm_b)

    row_bias, halves = lax.optimization_barrier((row_lse * (-1.0 / KAPPA), halves))
    col_lse, tile_max, kept = [], [], []
    for h, part in enumerate(halves):
        state, top, p = lse_call(whole_a, part, row_bias, keep=True, staged=h + 1 == HALVES)
        col_lse.append(group_lse(state, *over_a))
        tile_max.append(top)
        kept.append(pltpu.with_memory_space_constraint(p, pltpu.VMEM))
    row_sums = None
    for h in range(HALVES):
        row_sums = row_sum_call(kept[h], tile_max[h], col_lse[h], row_sums)
    row_sums = group_sum(row_sums, *over_b)
    col_sums = []
    for h in range(HALVES):
        sums = col_sum_call(kept[h], tile_max[h], col_lse[h], row_sums)
        col_sums.append(group_sum(sums, *over_a))

    def half_norms(h):
        return jnp.concatenate(norms_b[h * per_half : (h + 1) * per_half], 1)

    def quick(_):
        second_a = potential_a_of(row_lse) - epsilon * jnp.log(row_sums)
        second_b = [
            potential_b_of(col_lse[h], half_norms(h)) - epsilon * jnp.log(col_sums[h][:, :half])
            for h in range(HALVES)
        ]
        return second_a, jnp.concatenate(second_b, 1)

    def exact(_):
        state = None
        for part, lse in zip(halves, col_lse):
            (state,) = lse_call(part, whole_a, lse * (-1.0 / KAPPA), state)
        again = group_lse(state, *over_b)
        second_b = []
        for h, part in enumerate(halves):
            (state,) = lse_call(whole_a, part, again * (-1.0 / KAPPA))
            second_b.append(potential_b_of(group_lse(state, *over_a), half_norms(h)))
        return potential_a_of(again), jnp.concatenate(second_b, 1)

    second_a, second_b = lax.cond(col_sums[-1][0, half] > 0.0, exact, quick, 0)
    return second_a.reshape(-1), second_b.reshape(-1)


def solution(mesh):
    in_specs = (P("ba", "aa"), P("aa", "ba"))
    out_specs = (P("aa"), P("ba"))
    return jax.shard_map(
        functools.partial(per_device, mesh.shape["aa"], mesh.shape["ba"]),
        mesh=mesh, in_specs=in_specs, out_specs=out_specs, check_vma=False,
    )
```

```python
import functools
import math

import jax
import jax.numpy as jnp
from jax import lax
from jax.experimental import pallas as pl
from jax.experimental.pallas import tpu as pltpu
from jax.sharding import PartitionSpec as P

NA = 28672
NB = 28672
TOKENS = 256
epsilon = 0.01

f32 = jnp.float32
bf16 = jnp.bfloat16
VMEM = pl.BlockSpec(memory_space=pltpu.VMEM)

KAPPA = math.log2(math.e) * 2.0 / (TOKENS * epsilon)
LN2 = math.log(2.0)
SMALLEST = 2.0**-60


def params(mib):
    return pltpu.CompilerParams(vmem_limit_bytes=mib << 20)


def lse_kernel(tm, tn, biased, chained, keep, staged, lhs_ref, rhs_ref, *rest):
    rest = list(rest)
    bias_ref = rest.pop(0) if biased else None
    state_in = rest.pop(0) if chained else None
    state_ref = rest.pop(0)
    norm_ref = None if biased else rest.pop(0)
    if keep:
        tile_max_ref, kept_ref = rest.pop(0), rest.pop(0)
    turned, wide, *blocks = rest
    if staged:
        sent = blocks.pop()
        stage = blocks.pop()
    row_tiles = lhs_ref.shape[1] // tm
    total = row_tiles * (rhs_ref.shape[1] // tn)
    sub = 64 if keep or tm % 128 else 128
    lanes = tn // 128

    @pl.loop(0, lhs_ref.shape[1] // 128, unroll=7)
    def _(g):
        rows = pl.ds(pl.multiple_of(g * 128, 128), 128)
        turned[rows, :] = lhs_ref[:, rows].T
        if biased:
            bias = bias_ref[:, rows]
        else:
            norm = jnp.sum(jnp.square(lhs_ref[:, rows].astype(f32)), 0, keepdims=True)
            norm_ref[:, rows] = norm
            bias = -0.5 * norm
        wide[rows, :] = jnp.broadcast_to(bias, (128, 128)).T

    def cols(n):
        return pl.ds(pl.multiple_of(n * tn, tn), tn)

    def product(n, t, block):
        rows = pl.ds(pl.multiple_of(t * tm, tm), tm)
        block[...] = jnp.dot(turned[rows, :], rhs_ref[:, cols(n)], preferred_element_type=f32)

    def scores(t, k, block):
        rows = pl.ds(pl.multiple_of(t * tm + k, 64), sub)
        return block[k : k + sub, :] + jnp.concatenate([wide[rows, :]] * lanes, 1)

    def raised(n, t, block, upper, total_sum):
        new = upper
        for k in range(0, tm, sub):
            x = scores(t, k, block)
            if keep:
                block[k : k + sub, :] = x
            new = jnp.maximum(new, x.reshape(sub // 8, 8, tn).max(0))
        row = new.max(0, keepdims=True)
        new = jnp.broadcast_to(row, (8, tn))
        return row, new, total_sum * jnp.exp2((upper - new) * KAPPA)

    def send(step, parity, half):
        n = step // row_tiles
        rows = pl.ds(pl.multiple_of((step - n * row_tiles) * tm, tm), tm)
        return pltpu.make_async_copy(
            stage.at[parity, half], kept_ref.at[rows, cols(n)], sent.at[parity, half]
        )

    def reduce_kept(n, t, block, upper, total_sum, slot):
        row, new, total_sum = raised(n, t, block, upper, total_sum)
        for k in range(0, tm, sub):
            rows = pl.ds(pl.multiple_of(t * tm + k, 64), sub)
            p = jnp.exp2((block[k : k + sub, :] - row) * KAPPA)
            total_sum = total_sum + p.reshape(sub // 8, 8, tn).sum(0)
            if staged:
                stage[slot[0], slot[1], k : k + sub, :] = p.astype(bf16)
            else:
                kept_ref[rows, cols(n)] = p.astype(bf16)
        tile_max_ref[pl.ds(t, 1), cols(n)] = row
        return new, total_sum

    def reduce_only(n, t, block, upper, total_sum, slot):
        row, new, total_sum = raised(n, t, block, upper, total_sum)
        for k in range(0, tm, sub):
            p = jnp.exp2(((scores(t, k, block) - row) * KAPPA).astype(bf16))
            for g in range(0, sub, 64):
                part = (p[g : g + 16] + p[g + 16 : g + 32]) + (p[g + 32 : g + 48] + p[g + 48 : g + 64])
                part = part.astype(f32)
                total_sum = total_sum + (part[:8] + part[8:])
        return new, total_sum

    reduce = reduce_kept if keep else reduce_only
    product(0, 0, blocks[0])
    first_sublane = lax.broadcasted_iota(jnp.int32, (8, tn), 0) == 0

    def pair(k, carry):
        upper, total_sum = carry
        if staged:
            @pl.when(k >= 2)
            def _():
                for half in range(2):
                    send(2 * k + half, k % 2, half).wait()

        for half in range(2):
            step = 2 * k + half
            n = step // row_tiles
            t = step - n * row_tiles
            after = jnp.minimum(step + 1, total - 1)
            n_after = after // row_tiles
            if chained:
                start = state_in[:, cols(n)]
                start_max = jnp.broadcast_to(start[:1], (8, tn))
                start_sum = jnp.where(first_sublane, jnp.broadcast_to(start[1:], (8, tn)), 0.0)
            else:
                start_max, start_sum = jnp.full((8, tn), -1e30, f32), jnp.zeros((8, tn), f32)
            upper = jnp.where(t == 0, start_max, upper)
            total_sum = jnp.where(t == 0, start_sum, total_sum)
            product(n_after, after - n_after * row_tiles, blocks[1 - half])
            upper, total_sum = reduce(n, t, blocks[half], upper, total_sum, (k % 2, half))
            state_ref[0:1, cols(n)] = upper[:1]
            state_ref[1:2, cols(n)] = jnp.sum(total_sum, 0, keepdims=True)
        if staged:
            for half in range(2):
                send(2 * k + half, k % 2, half).start()
        return upper, total_sum

    zeros = jnp.zeros((8, tn), f32)
    lax.fori_loop(0, total // 2, pair, (zeros, zeros))
    if staged:
        for step in range(4):
            send(step, step // 2, step % 2).wait()


def lse_call(lhs, rhs, bias=None, state=None, keep=False, staged=False):
    depth, m = lhs.shape
    n = rhs.shape[1]
    tm, tn = (896, 512) if n % 512 == 0 else (448, 896)
    outs = [jax.ShapeDtypeStruct((2, n), f32)]
    operands = [lhs, rhs]
    if bias is None:
        outs += [jax.ShapeDtypeStruct((1, m), f32)]
    else:
        operands += [bias]
    if state is not None:
        operands += [state]
    if keep:
        place = pltpu.HBM if staged else pltpu.VMEM
        outs += [jax.ShapeDtypeStruct((m // tm, n), f32), place((m, n), bf16)]
    return pl.pallas_call(
        functools.partial(lse_kernel, tm, tn, bias is not None, state is not None, keep, staged),
        out_shape=outs,
        in_specs=[VMEM] * len(operands),
        out_specs=[VMEM] * (len(outs) - 1) + [pl.BlockSpec(memory_space=pltpu.HBM) if staged else VMEM],
        scratch_shapes=[pltpu.VMEM((m, depth), bf16), pltpu.VMEM((m, 128), f32)]
        + [pltpu.VMEM((tm, tn), f32)] * 2
        + ([pltpu.VMEM((2, 2, tm, tn), bf16), pltpu.SemaphoreType.DMA((2, 2))] if staged else []),
        compiler_params=params(14 if staged else 9 if keep else 12),
        cost_estimate=pl.CostEstimate(flops=512 * m * n, bytes_accessed=512 * (m + n), transcendentals=m * n),
    )(*operands)


def reorder_kernel(tokens, table_ref, arrived_ref, out_ref, norm_ref):
    for p in range(table_ref.shape[0]):
        start = pl.multiple_of(table_ref[p] * tokens, tokens)
        out_ref[p * tokens : (p + 1) * tokens, :] = arrived_ref[pl.ds(start, tokens), :]

    @pl.loop(0, arrived_ref.shape[1] // 128, unroll=7)
    def _(g):
        cols = pl.ds(pl.multiple_of(g * 128, 128), 128)
        norm_ref[:, cols] = jnp.sum(jnp.square(arrived_ref[:, cols].astype(f32)), 0, keepdims=True)


def reorder_call(arrived, table, tokens):
    return pl.pallas_call(
        functools.partial(reorder_kernel, tokens),
        out_shape=[
            jax.ShapeDtypeStruct(arrived.shape, bf16),
            jax.ShapeDtypeStruct((1, arrived.shape[1]), f32),
        ],
        in_specs=[pl.BlockSpec(memory_space=pltpu.SMEM), VMEM],
        out_specs=[VMEM] * 2,
        compiler_params=params(8),
    )(table, arrived)


def weights(tile_max_ref, lse_ref, t):
    return jnp.exp2(KAPPA * tile_max_ref[pl.ds(t, 1), :] - lse_ref[...])


def row_sum_kernel(chained, kept_ref, tile_max_ref, lse_ref, *rest):
    rest = list(rest)
    first = rest.pop(0) if chained else None
    out_ref, wide, partial = rest
    rows_here, cols_here = kept_ref.shape
    tiles = tile_max_ref.shape[0]
    tm = rows_here // tiles
    span, lane_block, height = 1024, 256, 64

    @pl.loop(0, tiles)
    def _(t):
        wide[...] = jnp.broadcast_to(weights(tile_max_ref, lse_ref, t), (16, cols_here)).astype(bf16)

        @pl.loop(0, tm // height, unroll=2 if tm % (2 * height) == 0 else 1)
        def _(g):
            rows = pl.ds(pl.multiple_of(t * tm + g * height, height), height)
            acc = jnp.zeros((height, 128), f32)
            for c in range(0, cols_here, span):
                part = None
                for k in range(c, min(c + span, cols_here), lane_block):
                    w = jnp.concatenate([wide[:, k : k + lane_block]] * (height // 16), 0)
                    term = kept_ref[rows, k : k + lane_block] * w
                    part = term if part is None else part + term
                part = part.astype(f32)
                for k in range(0, lane_block, 128):
                    acc = acc + part[:, k : k + 128]
            partial[rows, :] = acc

    @pl.loop(0, rows_here // 128, unroll=7)
    def _(g):
        rows = pl.ds(pl.multiple_of(g * 128, 128), 128)
        total = jnp.sum(partial[rows, :].T, axis=0, keepdims=True)
        out_ref[:, rows] = first[:, rows] + total if chained else total


def row_sum_call(kept, tile_max, lse, first=None):
    operands = (kept, tile_max, lse) if first is None else (kept, tile_max, lse, first)
    m, n = kept.shape
    return pl.pallas_call(
        functools.partial(row_sum_kernel, first is not None),
        out_shape=jax.ShapeDtypeStruct((1, m), f32),
        in_specs=[VMEM] * len(operands),
        out_specs=VMEM,
        scratch_shapes=[pltpu.VMEM((16, n), bf16), pltpu.VMEM((m, 128), f32)],
        compiler_params=params(3),
        cost_estimate=pl.CostEstimate(flops=2 * m * n, bytes_accessed=2 * m * n, transcendentals=0),
    )(*operands)


def col_sum_kernel(kept_ref, tile_max_ref, lse_ref, row_sum_ref, out_ref, wide):
    rows_here, cols_here = kept_ref.shape
    tiles = tile_max_ref.shape[0]
    tm = rows_here // tiles
    width = 896

    @pl.loop(0, rows_here // 128, unroll=7)
    def _(g):
        rows = pl.ds(pl.multiple_of(g * 128, 128), 128)
        scale = 1.0 / jnp.maximum(row_sum_ref[:, rows], SMALLEST)
        wide[rows, :] = jnp.broadcast_to(scale, (128, 128)).T.astype(bf16)

    least = jnp.min(row_sum_ref[...], axis=1, keepdims=True)
    out_ref[:, cols_here:] = jnp.broadcast_to(jnp.where(least < SMALLEST, 1.0, 0.0), (1, 128))

    @pl.loop(0, cols_here // width)
    def _(n):
        start = pl.multiple_of(n * width, 128)

        def tile(t, total):
            acc = jnp.zeros((16, width), f32)
            for g in range(tm // 64):
                part = None
                for h in range(4):
                    rows = pl.ds(pl.multiple_of(t * tm + g * 64 + h * 16, 16), 16)
                    scale = jnp.concatenate([wide[rows, :]] * (width // 128), 1)
                    term = kept_ref[rows, pl.ds(start, width)] * scale
                    part = term if part is None else part + term
                acc = acc + part.astype(f32)
            acc = jnp.sum(acc, 0, keepdims=True)
            cols = pl.ds(start, width)
            return total + acc * jnp.exp2(KAPPA * tile_max_ref[pl.ds(t, 1), cols] - lse_ref[:, cols])

        out_ref[:, pl.ds(start, width)] = lax.fori_loop(0, tiles, tile, jnp.zeros((1, width), f32))


def col_sum_call(kept, tile_max, lse, row_sums):
    m, n = kept.shape
    return pl.pallas_call(
        col_sum_kernel,
        out_shape=jax.ShapeDtypeStruct((1, n + 128), f32),
        in_specs=[VMEM] * 4,
        out_specs=VMEM,
        scratch_shapes=[pltpu.VMEM((m, 128), bf16)],
        compiler_params=params(3),
        cost_estimate=pl.CostEstimate(flops=2 * m * n, bytes_accessed=2 * m * n, transcendentals=0),
    )(kept, tile_max, lse, row_sums)


def near_first(near):
    return [[1 << k] for k in range(near.bit_length() - 1)] + [[near, 2 * near, 3 * near]]


def pairwise(size):
    return [[1 << k] for k in range(size.bit_length() - 1)]


def add_in_pairs(values):
    while len(values) > 1:
        values = [values[k] + values[k + 1] for k in range(0, len(values), 2)]
    return values[0]


def merge_kernel(last, *refs):
    *in_refs, out_ref = refs
    pairs = [ref[...] for ref in in_refs]
    top = functools.reduce(jnp.maximum, [pair[:1] for pair in pairs])
    total = add_in_pairs([pair[1:] * jnp.exp2((pair[:1] - top) * KAPPA) for pair in pairs])
    if last:
        out_ref[...] = KAPPA * top + jnp.log2(total)
    else:
        out_ref[0:1, :] = top
        out_ref[1:2, :] = total


def add_kernel(*refs):
    *in_refs, out_ref = refs
    out_ref[...] = add_in_pairs([ref[...] for ref in in_refs])


def small_call(kernel, shape, *operands):
    return pl.pallas_call(
        kernel,
        out_shape=jax.ShapeDtypeStruct(shape, f32),
        in_specs=[VMEM] * len(operands),
        out_specs=VMEM,
        compiler_params=params(1),
    )(*operands)


def swap(x, axis, size, mask):
    return lax.ppermute(x, axis, [(i, i ^ mask) for i in range(size)])


def group_lse(pair, axis, size, steps):
    for k, masks in enumerate(steps):
        last = k + 1 == len(steps)
        shape = (1 if last else 2, pair.shape[1])
        others = [swap(pair, axis, size, mask) for mask in masks]
        pair = small_call(functools.partial(merge_kernel, last), shape, pair, *others)
    return pair


def group_sum(x, axis, size, steps):
    for masks in steps:
        x = small_call(add_kernel, x.shape, x, *[swap(x, axis, size, mask) for mask in masks])
    return x


def gather_order(size, near):
    far = size // near
    return [f * near + k for k in range(near) for f in range(far)]


def after(x, other):
    return lax.optimization_barrier((x, other))[0]


CHUNKS = 4
HALVES = 2


def per_device(aa_size, ba_size, acts_a, acts_b):
    cols_here = acts_b.shape[1]
    width = cols_here // CHUNKS
    half = cols_here // HALVES
    near = aa_size // 4
    far_masks = [f * near for f in range(1, 4)]
    over_a = ("aa", aa_size, near_first(near))
    over_b = ("ba", ba_size, pairwise(ba_size))

    tokens = acts_b.shape[0]
    per_block = aa_size // ba_size
    arrival = gather_order(ba_size, 2)
    place = jnp.array([arrival.index(v) for v in range(ba_size)], jnp.int32)
    token_block = lax.axis_index("aa") ^ jnp.array(gather_order(aa_size, near), jnp.int32)
    table = place[(token_block // per_block) ^ lax.axis_index("ba")] * per_block + token_block % per_block
    group = [acts_a] + [swap(acts_a, "ba", ba_size, mask) for mask in range(2, ba_size, 2)]
    far_a = jnp.concatenate(group, 0)
    arrived_a = jnp.concatenate([far_a, swap(far_a, "ba", ba_size, 1)], 0)
    whole_a, norm_a = reorder_call(arrived_a, table, tokens)

    chunks, norms_b, states, sides = [], [], [], []

    def start_chunk(c):
        own = acts_b[:, c * width : (c + 1) * width]
        if c:
            own = after(own, sides[c - 1] if c >= 2 else far_a)
        group = [own] + [swap(own, "aa", aa_size, mask) for mask in far_masks]
        first = states[c - 2] if c >= 2 else far_a
        group = [own] + [after(piece, first) for piece in group[1:]]
        mine = jnp.concatenate(group, 0)
        sides.append(mine)
        return [mine] + [swap(mine, "aa", aa_size, k) for k in range(1, near)]

    coming = start_chunk(0)
    for c in range(CHUNKS):
        group = coming
        first = states[c - 1] if c else whole_a
        group = group[:1] + [after(piece, first) for piece in group[1:]]
        chunk = jnp.concatenate(group, 0)
        chunks.append(chunk)
        if c + 1 < CHUNKS:
            coming = start_chunk(c + 1)
            chunk = after(chunk, sides[c + 1])
        state, norm = lse_call(chunk, whole_a, None, states[c - 1] if c else None)
        states.append(state)
        norms_b.append(norm)
    row_lse = group_lse(states[-1], *over_b)
    per_half = CHUNKS // HALVES
    halves = [jnp.concatenate(chunks[h * per_half : (h + 1) * per_half], 1) for h in range(HALVES)]
    log_n = math.log(NA)

    def potential_a_of(row_lse):
        return -epsilon * (log_n + LN2 * (row_lse - (0.5 * KAPPA) * norm_a))

    def potential_b_of(col_lse, norm_b):
        return -epsilon * LN2 * (col_lse - (0.5 * KAPPA) * norm_b)

    row_bias, halves = lax.optimization_barrier((row_lse * (-1.0 / KAPPA), halves))
    col_lse, tile_max, kept = [], [], []
    for h, part in enumerate(halves):
        state, top, p = lse_call(whole_a, part, row_bias, keep=True, staged=h + 1 == HALVES)
        col_lse.append(group_lse(state, *over_a))
        tile_max.append(top)
        kept.append(pltpu.with_memory_space_constraint(p, pltpu.VMEM))
    row_sums = None
    for h in range(HALVES):
        row_sums = row_sum_call(kept[h], tile_max[h], col_lse[h], row_sums)
    row_sums = group_sum(row_sums, *over_b)
    col_sums = []
    for h in range(HALVES):
        sums = col_sum_call(kept[h], tile_max[h], col_lse[h], row_sums)
        col_sums.append(group_sum(sums, *over_a))

    def half_norms(h):
        return jnp.concatenate(norms_b[h * per_half : (h + 1) * per_half], 1)

    def quick(_):
        second_a = potential_a_of(row_lse) - epsilon * jnp.log(row_sums)
        second_b = [
            potential_b_of(col_lse[h], half_norms(h)) - epsilon * jnp.log(col_sums[h][:, :half])
            for h in range(HALVES)
        ]
        return second_a, jnp.concatenate(second_b, 1)

    def exact(_):
        state = None
        for part, lse in zip(halves, col_lse):
            (state,) = lse_call(part, whole_a, lse * (-1.0 / KAPPA), state)
        again = group_lse(state, *over_b)
        second_b = []
        for h, part in enumerate(halves):
            (state,) = lse_call(whole_a, part, again * (-1.0 / KAPPA))
            second_b.append(potential_b_of(group_lse(state, *over_a), half_norms(h)))
        return potential_a_of(again), jnp.concatenate(second_b, 1)

    second_a, second_b = lax.cond(col_sums[-1][0, half] > 0.0, exact, quick, 0)
    return second_a.reshape(-1), second_b.reshape(-1)


def solution(mesh):
    in_specs = (P("ba", "aa"), P("aa", "ba"))
    out_specs = (P("aa"), P("ba"))
    return jax.shard_map(
        functools.partial(per_device, mesh.shape["aa"], mesh.shape["ba"]),
        mesh=mesh, in_specs=in_specs, out_specs=out_specs, check_vma=False,
    )
```
